256 devices in a mesh: seq: 32 (over y, x, core), mp: 8 (over z).
Axes of the slice: x: 4, y: 4, z: 8, core: 2. Of those that a mesh axis runs over, the one named last changes fastest.
Arguments:
- hidden_rows: bfloat16 [4096, 8192], P('seq', 'mp'), may hold values from -6 to 6
- rotated_queries: bfloat16 [4096, 8192], P('seq', 'mp'), may hold values from -80 to 80
- rotated_keys: bfloat16 [4096, 1024], P('seq', 'mp'), may hold values from -6 to 6
- value_rows: bfloat16 [4096, 1024], P('seq', 'mp'), may hold values from -6 to 6
- adapter_down: bfloat16 [32, 16, 8192], P(None, None, 'mp'), may hold values from -0.0625 to 0.0625
- adapter_up: bfloat16 [32, 16, 8192], P(None, None, 'mp'), may hold values from -1.5 to 1.5
- output_gradient: bfloat16 [4096, 8192], P('seq', 'mp'), may hold values from -6 to 6
- document_blocks: int32 [9], replicated, may hold values from 1 to 17, 32 in all
- document_adapter: int32 [9], replicated, may hold values from 0 to 31
Outputs:
- attn_out: bfloat16 [4096, 8192], P('seq', 'mp')
- grad_q: bfloat16 [4096, 8192], P('seq', 'mp')
- grad_k: bfloat16 [4096, 1024], P('seq', 'mp')
- grad_v: bfloat16 [4096, 1024], P('seq', 'mp')
- grad_a: float32 [32, 16, 8192], P('seq', None, 'mp')
- grad_b: float32 [32, 16, 8192], P('seq', None, 'mp')
The draws below stay inside these ranges and needn't reach their ends.
All inputs are finite; a program needn't handle non-finite values.
Results may differ from the reference program's by a relative error of at most 0.02.
Values may be sent and summed in bfloat16 or wider, within the bound.
A program may use at most 128 MiB of HBM per device.

```python
import math
import jax
import jax.numpy as jnp
import numpy as np
from jax import lax

MODEL_WIDTH = 8192
QUERY_HEADS = 64
KV_HEADS = 8
HEAD_WIDTH = 128
ADAPTER_RANK = 16
BLK = 128
MAXB = 17
BLOCKS = 32
TOKENS = 4096
DOCS = 9
ADAPTER_COUNT = 32


def shared_keys(key):
    return jnp.clip(jax.random.normal(key, (TOKENS, KV_HEADS * HEAD_WIDTH), jnp.float32), -6.0, 6.0)


def draw_rotated_keys(key, part):
    base = shared_keys(key)
    return base.astype(jnp.bfloat16)


def draw_rotated_queries(key, part):
    key = jax.random.fold_in(key, 7)
    noise = jnp.clip(jax.random.normal(key, (TOKENS, QUERY_HEADS * HEAD_WIDTH), jnp.float32), -6.0, 6.0)
    return noise.astype(jnp.bfloat16)


def set_ends(array, stream_key, smallest, high):
    dims = array.shape
    spot = [jax.random.randint(jax.random.fold_in(stream_key, axis), (), 0, dims[axis]) for axis in range(len(dims))]
    array = array.at[tuple(spot)].set(smallest)
    longest = dims.index(max(dims))
    spot[longest] = (spot[longest] + 1) % dims[longest]
    return array.at[tuple(spot)].set(high)


def level_of(stream_key, dims, split, smallest, largest):
    factor_of = 1.0
    for dim, shards_of in split:
        steps = jax.random.uniform(jax.random.fold_in(jax.random.fold_in(stream_key, 6), dim), (shards_of,), jnp.float32, smallest / len(split), largest / len(split))
        factor_of = factor_of * jnp.repeat(jnp.exp(steps), dims[dim] // shards_of).reshape((-1,) + (1,) * (len(dims) - 1 - dim))
    return factor_of


def profile(count, total, bound, skew):
    portions = [(1 << 20) // math.isqrt(grade ** skew) + 1 for grade in range(2, count + 1)]
    rest, counts = total - bound - (count - 1), [1] * (count - 1)
    while rest > 0:
        free = [i for i in range(count - 1) if counts[i] < bound]
        mass, budget = sum([portions[i] for i in free]), rest
        for i in free:
            addition = min(bound - counts[i], max(1, budget * portions[i] // mass), rest)
            counts[i] = counts[i] + addition
            rest = rest - addition
    return np.array([bound] + counts)


def uneven(key, count, total, most, slope):
    if count == 2:
        one = jax.random.randint(key, (), max(1, total - most), min(most, total - 1) + 1)
        return jnp.stack([one, total - one])
    tallies = jnp.asarray(profile(count, total, most, slope), jnp.int32)
    twos = (count - 1) // 2
    giver, sink = tallies[1:1 + 2 * twos:2], tallies[2:2 + 2 * twos:2]
    slack = jnp.minimum(giver - 1, most - sink)
    moved = jax.random.randint(jax.random.fold_in(key, 1), (twos,), 0, 1 << 20) % (slack + 1)
    tallies = tallies.at[1:1 + 2 * twos:2].set(giver - moved).at[2:2 + 2 * twos:2].set(sink + moved)
    return tallies[jax.random.permutation(jax.random.fold_in(key, 2), count)]


def gaussian(rng, extent, scale, reach, shards=(), held_as=jnp.bfloat16):
    drawn = scale * jax.random.normal(rng, extent, jnp.float32)
    if shards:
        drawn = drawn * level_of(rng, extent, shards, -0.22, 0.18)
    return jnp.clip(drawn, -reach, reach).astype(held_as)


def setup_inputs(seed: int = 0) -> dict:
    splits = jax.random.split(jax.random.key(seed), 10)
    hidden_rows = gaussian(splits[0], (TOKENS, MODEL_WIDTH), 1.0, 6.0, ((0, 32), (1, 8)))
    rotated_queries = draw_rotated_queries(jax.random.fold_in(splits[9], 71), 0)
    rotated_keys = draw_rotated_keys(jax.random.fold_in(splits[9], 71), 0)
    value_rows = gaussian(splits[3], (TOKENS, KV_HEADS * HEAD_WIDTH), 1.0, 6.0, ((0, 32), (1, 8)))
    adapter_down = gaussian(splits[4], (ADAPTER_COUNT, ADAPTER_RANK, MODEL_WIDTH), MODEL_WIDTH ** -0.5, 0.0625, ((2, 8),))
    adapter_up = gaussian(splits[5], (ADAPTER_COUNT, ADAPTER_RANK, QUERY_HEADS * HEAD_WIDTH), ADAPTER_RANK ** -0.5, 1.5, ((2, 8),))
    output_gradient = gaussian(splits[6], (TOKENS, QUERY_HEADS * HEAD_WIDTH), 1.0, 6.0, ((0, 32), (1, 8)))
    document_blocks = uneven(splits[7], DOCS, BLOCKS, MAXB, 2).astype(jnp.int32)
    document_adapter = set_ends(jax.random.randint(splits[8], (DOCS,), 0, ADAPTER_COUNT), jax.random.fold_in(splits[8], 1), 0, ADAPTER_COUNT - 1).astype(jnp.int32)
    return {"hidden_rows": hidden_rows, "rotated_queries": rotated_queries, "rotated_keys": rotated_keys, "value_rows": value_rows, "adapter_down": adapter_down, "adapter_up": adapter_up, "output_gradient": output_gradient, "document_blocks": document_blocks, "document_adapter": document_adapter}


def block_documents(document_blocks, count):
    ends = jnp.cumsum(document_blocks)
    blocks = jnp.arange(count, dtype=jnp.int32)
    return lax.optimization_barrier(jnp.sum((blocks[:, None] >= ends[None, :]).astype(jnp.int32), axis=1))

def pick(table, index):
    places = jnp.arange(table.shape[0], dtype=jnp.int32)
    return jnp.sum(jnp.where(places == index, table, 0))

def window_mask(same, rows):
    places = jnp.arange(rows, dtype=jnp.int32)
    causal = places[None, :] <= places[:, None]
    parts = [jnp.logical_and(causal, same[0])]
    for dist in range(1, same.shape[0]):
        parts.append(jnp.broadcast_to(same[dist], (rows, rows)))
    return jnp.concatenate(parts, axis=1)

def attend(query, window, allowed, output_gradient, scale):
    rows = query.shape[0]
    kv_cols = window.shape[2]
    groups = kv_cols // HEAD_WIDTH
    ratio = query.shape[1] // kv_cols
    q_four = query.reshape(rows, groups, ratio, HEAD_WIDTH).astype(jnp.float32)
    keys = window[:, 0].reshape(-1, groups, HEAD_WIDTH).astype(jnp.float32)
    values = window[:, 1].reshape(-1, groups, HEAD_WIDTH).astype(jnp.float32)
    scores = jnp.einsum('tgjd,ugd->gjtu', q_four, keys) * scale
    scores = jnp.where(allowed[None, None], scores, -1e+30)
    top = lax.optimization_barrier(jnp.max(scores, axis=-1, keepdims=True))
    lse = top + jnp.log(lax.optimization_barrier(jnp.sum(jnp.exp(scores - top), axis=-1, keepdims=True)))
    probs = jnp.exp(scores - lse)
    probs_b = probs.astype(jnp.bfloat16)
    out = jnp.einsum('gjtu,ugd->tgjd', probs_b.astype(jnp.float32), values).astype(jnp.bfloat16)
    grad_four = output_gradient.reshape(rows, groups, ratio, HEAD_WIDTH).astype(jnp.float32)
    delta = lax.optimization_barrier(jnp.sum(grad_four * out.astype(jnp.float32), axis=-1))
    delta = jnp.transpose(delta, (1, 2, 0))[..., None]
    dprob = jnp.einsum('tgjd,ugd->gjtu', grad_four, values)
    dscore = (probs * (dprob - delta)).astype(jnp.bfloat16).astype(jnp.float32)
    grad_query = (jnp.einsum('gjtu,ugd->tgjd', dscore, keys) * scale).astype(jnp.bfloat16)
    grad_keys = jnp.einsum('gjtu,tgjd->ugd', dscore, q_four) * scale
    grad_values = jnp.einsum('gjtu,tgjd->ugd', probs_b.astype(jnp.float32), grad_four)
    both = jnp.stack((grad_keys.reshape(-1, kv_cols), grad_values.reshape(-1, kv_cols)), axis=1)
    return (out.reshape(rows, -1), grad_query.reshape(rows, -1), both)

def reference(hidden_rows, rotated_queries, rotated_keys, value_rows, adapter_down, adapter_up, output_gradient, document_blocks, document_adapter):
    scale = 1.0 / math.sqrt(HEAD_WIDTH)
    docs = block_documents(document_blocks, BLOCKS)
    doc_places = jnp.arange(document_adapter.shape[0], dtype=jnp.int32)
    block_adapter = lax.optimization_barrier(jnp.sum(jnp.where(docs[:, None] == doc_places[None, :], document_adapter[None, :], 0), axis=1))
    token_adapter = jnp.repeat(block_adapter, BLK)
    choose = token_adapter[:, None] == jnp.arange(ADAPTER_COUNT, dtype=jnp.int32)[None, :]
    choose_f = choose.astype(jnp.float32)
    choose_b = choose.astype(jnp.bfloat16)
    down_flattened = adapter_down.reshape(ADAPTER_COUNT * ADAPTER_RANK, MODEL_WIDTH)
    up_flattened = adapter_up.reshape(ADAPTER_COUNT * ADAPTER_RANK, QUERY_HEADS * HEAD_WIDTH)
    low_all = jnp.dot(hidden_rows, down_flattened.T, preferred_element_type=jnp.float32).reshape(TOKENS, ADAPTER_COUNT, ADAPTER_RANK)
    low = lax.optimization_barrier(jnp.sum(low_all * choose_f[:, :, None], axis=1)).astype(jnp.bfloat16)
    spread = (choose_b[:, :, None] * low[:, None, :]).reshape(TOKENS, ADAPTER_COUNT * ADAPTER_RANK)
    query = (rotated_queries.astype(jnp.float32) + jnp.dot(spread, up_flattened, preferred_element_type=jnp.float32)).astype(jnp.bfloat16)
    width = KV_HEADS * HEAD_WIDTH
    lead = (MAXB - 1) * BLK
    stacked = jnp.stack((rotated_keys, value_rows), axis=1)
    padded = jnp.concatenate((jnp.zeros((lead, 2, width), jnp.bfloat16), stacked), axis=0)
    start_acc = jnp.zeros((lead + TOKENS, 2, width), jnp.float32)

    def step(acc, block):
        block = block.astype(jnp.int32)
        doc_own = pick(docs, block)
        q_block = lax.dynamic_slice_in_dim(query, block * BLK, BLK, 0)
        g_block = lax.dynamic_slice_in_dim(output_gradient, block * BLK, BLK, 0)
        pieces = []
        same = []
        for dist in range(MAXB):
            start = (block - dist + MAXB - 1) * BLK
            pieces.append(lax.dynamic_slice_in_dim(padded, start, BLK, 0))
            same.append(jnp.logical_and(block - dist >= 0, pick(docs, block - dist) == doc_own))
        window = jnp.concatenate(pieces, axis=0)
        allowed = window_mask(jnp.stack(same), BLK)
        out, grad_query, both = attend(q_block, window, allowed, g_block, scale)
        for dist in range(MAXB):
            start = (block - dist + MAXB - 1) * BLK
            part = lax.dynamic_slice_in_dim(acc, start, BLK, 0)
            acc = lax.dynamic_update_slice_in_dim(acc, part + both[dist * BLK:(dist + 1) * BLK], start, 0)
        return (acc, (out, grad_query))
    acc, (outs, grads) = lax.scan(step, start_acc, jnp.arange(BLOCKS, dtype=jnp.int32))
    attn_out = outs.reshape(TOKENS, QUERY_HEADS * HEAD_WIDTH)
    grad_q = grads.reshape(TOKENS, QUERY_HEADS * HEAD_WIDTH)
    key_value = acc[lead:]
    grad_k = key_value[:, 0].astype(jnp.bfloat16)
    grad_v = key_value[:, 1].astype(jnp.bfloat16)
    dlow_all = jnp.dot(grad_q, up_flattened.T, preferred_element_type=jnp.float32).reshape(TOKENS, ADAPTER_COUNT, ADAPTER_RANK)
    dlow = lax.optimization_barrier(jnp.sum(dlow_all * choose_f[:, :, None], axis=1)).astype(jnp.bfloat16)
    spread_d = (choose_b[:, :, None] * dlow[:, None, :]).reshape(TOKENS, ADAPTER_COUNT * ADAPTER_RANK)
    grad_a = jnp.dot(spread_d.T, hidden_rows, preferred_element_type=jnp.float32).reshape(ADAPTER_COUNT, ADAPTER_RANK, MODEL_WIDTH)
    grad_b = jnp.dot(spread.T, grad_q, preferred_element_type=jnp.float32).reshape(ADAPTER_COUNT, ADAPTER_RANK, QUERY_HEADS * HEAD_WIDTH)
    return (attn_out, grad_q, grad_k, grad_v, grad_a, grad_b)
```

```python
import functools
import math

import jax
import jax.numpy as jnp
from jax import lax
from jax.experimental import pallas as pl
from jax.experimental.pallas import tpu as pltpu
from jax.sharding import PartitionSpec as P

HEAD = 128
BLK = 128
RANK = 16
CHUNK = 256
NEG = -1e30
LOG2E = 1.4426950408889634
MESH = pl.DeviceIdType.MESH
F32 = jnp.float32
BF16 = jnp.bfloat16

NT = (((1,), (1,)), ((), ()))


def dot(a, b):
    return jnp.dot(a, b, preferred_element_type=F32)


def dot_nt(a, b):
    return lax.dot_general(a, b, NT, preferred_element_type=F32)


def kernel(
    seq, mp, docs,
    db, da, hid_h, rq_h, k_h, v_h, down_h, up_h, do_h,
    out_h, gq_h, gk_h, gv_h, ga_h, gb_h,
    hid, rq, down, up, do, kv, qs, dos, sbuf, dpbuf,
    lowx, dlowx, stat, ot, dqt, outv, gqv, pair, own_st, sib_out, sib_in,
    dkv_out, dkv_in, gkv, select, piece, got, red, fin, gout,
    load_sem, out_sem,
    low_send, low_recv, dlow_send, dlow_recv,
    kv_send, kv_recv, fwd_send, fwd_recv, sib_send, sib_recv, dkv_send, dkv_recv,
    a1_send, a1_recv, a2_send, a2_recv,
):
    reach = seq // 4
    chips = seq // 2
    cols = hid.shape[1]
    heads = cols // HEAD
    chunks = cols // CHUNK
    per = CHUNK // HEAD
    scale = 1.0 / math.sqrt(HEAD)
    fold = scale * LOG2E

    own = lax.axis_index("seq")
    m = lax.axis_index("mp")
    chip = own // 2
    core = own % 2
    sib = own + 1 - 2 * core
    mine = pl.ds(pl.multiple_of(core * BLK, BLK), BLK)
    other = pl.ds(pl.multiple_of((1 - core) * BLK, BLK), BLK)

    def load(src, dst, n):
        return pltpu.make_async_copy(src, dst, load_sem.at[n])

    loads = [
        load(k_h, kv.at[0, 0, mine], 0),
        load(v_h, kv.at[0, 1, mine], 1),
        load(hid_h, hid, 2),
        load(down_h, down, 3),
        load(up_h, up, 4),
        load(rq_h, rq, 5),
        load(do_h, do, 6),
    ]
    for one in loads:
        one.start()

    barrier = pltpu.get_barrier_semaphore()

    @pl.loop(1, seq)
    def _(step):
        pl.semaphore_signal(
            barrier, inc=1, device_id=((own + step) % seq, m), device_id_type=MESH
        )

    for step in range(1, mp):
        pl.semaphore_signal(
            barrier, inc=1, device_id=(own, (m + step) % mp), device_id_type=MESH
        )

    start = jnp.int32(0)
    first = jnp.int32(0)
    adapter = jnp.int32(0)
    bounds = []
    for d in range(docs):
        end = start + db[d]
        inside = jnp.logical_and(own >= start, own < end)
        first = jnp.where(inside, start, first)
        adapter = jnp.where(inside, da[d], adapter)
        bounds.append((start, end, da[d]))
        start = end

    loads[2].wait()
    loads[3].wait()
    lowx[m] = dot_nt(down[adapter], hid[...])
    loads[0].wait()
    loads[1].wait()

    pl.semaphore_wait(barrier, seq - 1 + mp - 1)

    def exchange(buf, send, recv):
        copies = []
        for step in range(1, mp):
            peer = (m + step) % mp
            copies.append(
                pltpu.make_async_remote_copy(
                    src_ref=buf.at[m], dst_ref=buf.at[m],
                    send_sem=send.at[step], recv_sem=recv.at[step],
                    device_id=(own, peer), device_id_type=MESH,
                )
            )
        return copies

    low_copies = exchange(lowx, low_send, low_recv)
    for one in low_copies:
        one.start()

    def kv_copy(e):
        return pltpu.make_async_remote_copy(
            src_ref=kv.at[0, :, mine], dst_ref=kv.at[e, :, mine],
            send_sem=kv_send.at[e], recv_sem=kv_recv.at[e],
            device_id=(own + 2 * e, m), device_id_type=MESH,
        )

    def kv_land(e):
        return pltpu.make_async_remote_copy(
            src_ref=kv.at[0, :, mine], dst_ref=kv.at[e, :, mine],
            send_sem=kv_send.at[e], recv_sem=kv_recv.at[e],
            device_id=(sib, m), device_id_type=MESH,
        )

    def forward(e):
        return pltpu.make_async_remote_copy(
            src_ref=kv.at[e, :, mine], dst_ref=kv.at[e, :, mine],
            send_sem=fwd_send.at[e], recv_sem=fwd_recv.at[e],
            device_id=(sib, m), device_id_type=MESH,
        )

    def forward_land(e):
        return pltpu.make_async_remote_copy(
            src_ref=kv.at[e, :, other], dst_ref=kv.at[e, :, other],
            send_sem=fwd_send.at[e], recv_sem=fwd_recv.at[e],
            device_id=(sib, m), device_id_type=MESH,
        )

    later = jnp.minimum(reach, chips - 1 - chip)
    earlier = jnp.minimum(reach, chip)

    forward(0).start()

    @pl.loop(1, later + 1)
    def _(e):
        kv_copy(e).start()

    loads[6].wait()
    for h in range(heads):
        dos[h * BLK : (h + 1) * BLK, :] = do[:, h * HEAD : (h + 1) * HEAD]

    wide = seq * 8
    row = lax.broadcasted_iota(jnp.int32, (wide, wide), 0)
    col = lax.broadcasted_iota(jnp.int32, (wide, wide), 1)
    same = (row % 8) == (col % 8)
    row_a = row // 8
    col_s = col // 8
    hit = jnp.zeros((wide, wide), F32)
    for begin, end, name in bounds:
        inside = jnp.logical_and(col_s >= begin, col_s < end)
        inside = jnp.logical_and(inside, row_a == name)
        hit = jnp.where(jnp.logical_and(inside, same), 1.0, hit)
    select[...] = hit.astype(BF16)

    loads[4].wait()
    loads[5].wait()
    for one in low_copies:
        one.wait_recv()
    low_sum = lowx[0]
    for step in range(1, mp):
        low_sum = low_sum + lowx[step]
    low_t = low_sum.astype(BF16)
    up_rows = up[adapter]
    low = low_sum.T.astype(BF16)
    for h in range(heads):
        part = slice(h * HEAD, (h + 1) * HEAD)
        q = rq[:, part].astype(F32) + dot(low, up_rows[:, part])
        qs[h * BLK : (h + 1) * BLK, :] = q.astype(BF16)

    u_rows = lax.broadcasted_iota(jnp.int32, (2 * BLK, CHUNK), 0)
    t_cols = lax.broadcasted_iota(jnp.int32, (2 * BLK, CHUNK), 1) % BLK

    def forward_unit(e, diagonal):
        low_edge = (first - 2 * (chip - e)) * BLK
        keys = kv[e, 0]
        values = kv[e, 1]
        values_t = values.T
        for ch in range(chunks):
            part = slice(ch * CHUNK, (ch + 1) * CHUNK)
            s = dot_nt(keys, qs[part, :])
            keep = u_rows >= low_edge
            if diagonal:
                keep = jnp.logical_and(keep, u_rows <= core * BLK + t_cols)
            s = jnp.where(keep, s, NEG)
            sbuf[e, :, part] = s
            dp = dot_nt(values, dos[part, :])
            dpbuf[e, :, part] = dp
            top = jnp.max(s, axis=0, keepdims=True)
            if not diagonal:
                was = stat[0:1, part]
                top = jnp.maximum(top, was)
            p = jnp.exp2(s * fold - top * fold)
            total = jnp.sum(p, axis=0, keepdims=True)
            delta = jnp.sum(p * dp, axis=0, keepdims=True)
            o = dot(values_t, p.astype(BF16))
            if not diagonal:
                shrink = jnp.exp2((was - top) * fold)
                total = total + shrink * stat[8:9, part]
                delta = delta + shrink * stat[16:17, part]
                o = o + shrink * ot[:, part]
            stat[0:1, part] = top
            stat[8:9, part] = total
            stat[16:17, part] = delta
            ot[:, part] = o

    forward_land(0).wait_recv()
    forward_unit(0, True)

    @pl.loop(1, earlier + 2)
    def _(e):
        @pl.when(e <= earlier)
        def _():
            kv_land(e).wait_recv()
            forward(e).start()

        @pl.when(e >= 2)
        def _():
            forward_land(e - 1).wait_recv()
            forward_unit(e - 1, False)

    total = stat[8:9, :]
    inverse = 1.0 / total
    stat[24:25, :] = stat[0:1, :] * fold + jnp.log(total) * LOG2E
    stat[16:17, :] = stat[16:17, :] * inverse
    for h in range(heads):
        part = slice(h * HEAD, (h + 1) * HEAD)
        outv[:, part] = (ot[:, part] * inverse[:, part]).T.astype(BF16)
    out_copy = pltpu.make_async_copy(outv, out_h, out_sem.at[0])
    out_copy.start()

    def sib_copy(e):
        return pltpu.make_async_remote_copy(
            src_ref=sib_out.at[e], dst_ref=sib_in.at[e],
            send_sem=sib_send.at[e], recv_sem=sib_recv.at[e],
            device_id=(sib, m), device_id_type=MESH,
        )

    def dkv_copy(e):
        return pltpu.make_async_remote_copy(
            src_ref=dkv_out.at[e], dst_ref=dkv_in.at[e],
            send_sem=dkv_send.at[e], recv_sem=dkv_recv.at[e],
            device_id=(own - 2 * e, m), device_id_type=MESH,
        )

    def dkv_land(e):
        return pltpu.make_async_remote_copy(
            src_ref=dkv_out.at[e], dst_ref=dkv_in.at[e],
            send_sem=dkv_send.at[e], recv_sem=dkv_recv.at[e],
            device_id=(sib, m), device_id_type=MESH,
        )

    dqt[...] = jnp.zeros_like(dqt)

    @pl.loop(0, earlier + 1)
    def _(turn):
        e = earlier - turn
        keys_t = kv[e, 0].T
        dk = jnp.zeros((2 * BLK, HEAD), F32)
        dv = jnp.zeros((2 * BLK, HEAD), F32)
        for ch in range(chunks):
            part = slice(ch * CHUNK, (ch + 1) * CHUNK)
            p = jnp.exp2(sbuf[e, :, part] * fold - stat[24:25, part])
            ds = (p * (dpbuf[e, :, part] - stat[16:17, part])).astype(BF16)
            dv = dv + dot(p.astype(BF16), dos[part, :])
            dk = dk + dot(ds, qs[part, :])
            dqt[:, part] = dqt[:, part] + dot(keys_t, ds)
        pair[0] = dk * scale
        pair[1] = dv
        own_st[e] = pair[:, mine, :]
        sib_out[e] = pair[:, other, :].astype(BF16)
        sib_copy(e).start()

        @pl.when(turn >= 1)
        def _():
            sib_copy(e + 1).wait_recv()
            dkv_out[e + 1] = (own_st[e + 1] + sib_in[e + 1].astype(F32)).astype(BF16)
            dkv_copy(e + 1).start()

    for h in range(heads):
        part = slice(h * HEAD, (h + 1) * HEAD)
        gqv[:, part] = (dqt[:, part] * scale).T.astype(BF16)
    dlowx[m] = dot_nt(up_rows, gqv[...])
    dlow_copies = exchange(dlowx, dlow_send, dlow_recv)
    for one in dlow_copies:
        one.start()
    gq_copy = pltpu.make_async_copy(gqv, gq_h, out_sem.at[1])
    gq_copy.start()

    half = seq // 2

    def a1_copy(index):
        return pltpu.make_async_remote_copy(
            src_ref=piece.at[index],
            dst_ref=got.at[pl.ds(pl.multiple_of(own * 8, 8), 8)],
            send_sem=a1_send, recv_sem=a1_recv,
            device_id=(index, m), device_id_type=MESH,
        )

    def spread(product, base):
        for t in range(cols // 128):
            for r in range(2):
                piece[base + t * 2 + r] = product[r * 8 : (r + 1) * 8, t * 128 : (t + 1) * 128]

        @pl.loop(0, half)
        def _(step):
            index = base + (own + step) % half

            @pl.when(index != own)
            def _():
                a1_copy(index).start()

    spread(dot(low_t, gqv[...]), 0)

    for one in dlow_copies:
        one.wait_recv()
    dlow_sum = dlowx[0]
    for step in range(1, mp):
        dlow_sum = dlow_sum + dlowx[step]
    spread(dot(dlow_sum.astype(BF16), hid[...]), half)
    mine8 = pl.ds(pl.multiple_of(own * 8, 8), 8)

    sib_copy(0).wait_recv()
    pair[:, 0:BLK, :] = own_st[0] + sib_in[0].astype(F32)

    @pl.loop(1, later + 1)
    def _(e):
        dkv_land(e).wait_recv()
        pair[:, 0:BLK, :] = pair[:, 0:BLK, :] + dkv_in[e].astype(F32)

    gkv[...] = pair[:, 0:BLK, :].astype(BF16)
    gk_copy = pltpu.make_async_copy(gkv.at[0], gk_h, out_sem.at[2])
    gv_copy = pltpu.make_async_copy(gkv.at[1], gv_h, out_sem.at[3])
    gk_copy.start()
    gv_copy.start()

    rest = (seq - 1) * 8
    pltpu.make_async_copy(got.at[pl.ds(0, rest)], got.at[pl.ds(0, rest)], a1_recv).wait()
    got[mine8, :] = piece[own]
    high = got[...].astype(BF16)
    tail = (got[...] - high.astype(F32)).astype(BF16)
    red[...] = dot(select[...], high) + dot(select[...], tail)

    @pl.loop(1, seq)
    def _(step):
        peer = (own + step) % seq
        pltpu.make_async_remote_copy(
            src_ref=red.at[pl.ds(pl.multiple_of(peer * 8, 8), 8)],
            dst_ref=fin.at[mine8],
            send_sem=a2_send, recv_sem=a2_recv,
            device_id=(peer, m), device_id_type=MESH,
        ).start()

    pltpu.make_async_copy(fin.at[pl.ds(0, rest)], fin.at[pl.ds(0, rest)], a2_recv).wait()
    fin[mine8, :] = red[mine8, :]
    for kind in range(2):
        for t in range(cols // 128):
            for r in range(2):
                at = (kind * half + t * 2 + r) * 8
                gout[kind, r * 8 : (r + 1) * 8, t * 128 : (t + 1) * 128] = fin[at : at + 8, :]
    gb_copy = pltpu.make_async_copy(gout.at[0], gb_h.at[0], out_sem.at[4])
    ga_copy = pltpu.make_async_copy(gout.at[1], ga_h.at[0], out_sem.at[5])
    gb_copy.start()
    ga_copy.start()

    for one in low_copies + dlow_copies:
        one.wait_send()

    @pl.loop(1, later + 1)
    def _(e):
        kv_copy(e).wait_send()

    @pl.loop(0, earlier + 1)
    def _(e):
        forward(e).wait_send()
        sib_copy(e).wait_send()

    @pl.loop(1, earlier + 1)
    def _(e):
        dkv_copy(e).wait_send()

    pltpu.make_async_copy(got.at[pl.ds(0, rest)], got.at[pl.ds(0, rest)], a1_send).wait()
    pltpu.make_async_copy(red.at[pl.ds(0, rest)], red.at[pl.ds(0, rest)], a2_send).wait()
    for one in (out_copy, gq_copy, gk_copy, gv_copy, ga_copy, gb_copy):
        one.wait()


def on_device(
    hidden_rows, rotated_queries, rotated_keys, value_rows, adapter_down, adapter_up,
    output_gradient, document_blocks, document_adapter,
):
    seq = lax.axis_size("seq")
    mp = lax.axis_size("mp")
    rows, cols = hidden_rows.shape
    adapters = adapter_down.shape[0]
    units = seq // 4 + 1
    any_space = pl.BlockSpec(memory_space=pl.ANY)
    smem = pl.BlockSpec(memory_space=pltpu.SMEM)
    dma = pltpu.SemaphoreType.DMA
    vmem = pltpu.VMEM
    return pl.pallas_call(
        functools.partial(kernel, seq, mp, document_blocks.shape[0]),
        out_shape=(
            jax.ShapeDtypeStruct((rows, cols), BF16),
            jax.ShapeDtypeStruct((rows, cols), BF16),
            jax.ShapeDtypeStruct((rows, HEAD), BF16),
            jax.ShapeDtypeStruct((rows, HEAD), BF16),
            jax.ShapeDtypeStruct((1, RANK, cols), F32),
            jax.ShapeDtypeStruct((1, RANK, cols), F32),
        ),
        in_specs=[smem, smem] + [any_space] * 7,
        out_specs=[any_space] * 6,
        scratch_shapes=[
            vmem((rows, cols), BF16),
            vmem((rows, cols), BF16),
            vmem((adapters, RANK, cols), BF16),
            vmem((adapters, RANK, cols), BF16),
            vmem((rows, cols), BF16),
            vmem((units, 2, 2 * BLK, HEAD), BF16),
            vmem((cols, HEAD), BF16),
            vmem((cols, HEAD), BF16),
            vmem((units, 2 * BLK, cols), F32),
            vmem((units, 2 * BLK, cols), F32),
            vmem((mp, RANK, rows), F32),
            vmem((mp, RANK, rows), F32),
            vmem((32, cols), F32),
            vmem((HEAD, cols), F32),
            vmem((HEAD, cols), F32),
            vmem((rows, cols), BF16),
            vmem((rows, cols), BF16),
            vmem((2, 2 * BLK, HEAD), F32),
            vmem((units, 2, BLK, HEAD), F32),
            vmem((units, 2, BLK, HEAD), BF16),
            vmem((units, 2, BLK, HEAD), BF16),
            vmem((units, 2, BLK, HEAD), BF16),
            vmem((units, 2, BLK, HEAD), BF16),
            vmem((2, BLK, HEAD), BF16),
            vmem((seq * 8, seq * 8), BF16),
            vmem((seq, 8, 128), F32),
            vmem((seq * 8, 128), F32),
            vmem((seq * 8, 128), F32),
            vmem((seq * 8, 128), F32),
            vmem((2, RANK, cols), F32),
            dma((7,)), dma((6,)),
            dma((mp,)), dma((mp,)), dma((mp,)), dma((mp,)),
            dma((units,)), dma((units,)), dma((units,)), dma((units,)),
            dma((units,)), dma((units,)), dma((units,)), dma((units,)),
            dma, dma, dma, dma,
        ],
        compiler_params=pltpu.CompilerParams(
            collective_id=0, has_side_effects=True, vmem_limit_bytes=48 * 1024 * 1024
        ),
    )(
        document_blocks, document_adapter, hidden_rows, rotated_queries, rotated_keys,
        value_rows, adapter_down, adapter_up, output_gradient,
    )


def solution(mesh):
    return jax.shard_map(
        on_device,
        mesh=mesh,
        in_specs=(
            P("seq", "mp"),
            P("seq", "mp"),
            P("seq", "mp"),
            P("seq", "mp"),
            P(None, None, "mp"),
            P(None, None, "mp"),
            P("seq", "mp"),
            P(),
            P(),
        ),
        out_specs=(
            P("seq", "mp"),
            P("seq", "mp"),
            P("seq", "mp"),
            P("seq", "mp"),
            P("seq", None, "mp"),
            P("seq", None, "mp"),
        ),
        check_vma=False,
    )
```

```python
import functools
import math

import jax
import jax.numpy as jnp
from jax import lax
from jax.experimental import pallas as pl
from jax.experimental.pallas import tpu as pltpu
from jax.sharding import PartitionSpec as P

HEAD = 128
BLK = 128
RANK = 16
CHUNK = 1024
NARROW = 256
GROUP = 3
LAG = 3
NEG = -1e30
LOG2E = 1.4426950408889634
MESH = pl.DeviceIdType.MESH
F32 = jnp.float32
BF16 = jnp.bfloat16

NT = (((1,), (1,)), ((), ()))


def dot(a, b):
    return jnp.dot(a, b, preferred_element_type=F32)


def dot_nt(a, b):
    return lax.dot_general(a, b, NT, preferred_element_type=F32)


def kernel(
    seq, mp, docs,
    db_h, da_h, hid_h, rq_h, k_h, v_h, down_h, up_h, do_h,
    out_h, gq_h, gk_h, gv_h, ga_h, gb_h,
    db, da, hid, rq, down, up, do, kv, qs, qt, dos, dot_t, sbuf, dpbuf, pbuf, dsbuf,
    lowx, dlowx, stat, keys_t, vals_t, outv, gqv, pair, own_st, sib_out, sib_in,
    dkv_out, dkv_in, home_out, home_in, gkv, total_kv, select, piece, got, red, fin, gout,
    load_sem, out_sem,
    low_send, low_recv, dlow_send, dlow_recv,
    col_send, row_send, kv_recv, fwd_send, fwd_recv, sib_send, sib_recv, dkv_send, dkv_recv,
    home_send, home_recv,
    a1_send, a1_recv, a2_send, a2_recv,
):
    reach = seq // 4
    chips = seq // 2
    units = reach + 1
    wide = reach // 2
    tall = chips // wide
    cols = hid.shape[1]
    heads = cols // HEAD
    span = cols // 128
    groups = units // GROUP
    scale = 1.0 / math.sqrt(HEAD)
    fold = scale * LOG2E

    own = lax.axis_index("seq")
    m = lax.axis_index("mp")
    chip = own // 2
    core = own % 2
    sib = own + 1 - 2 * core
    place = own % span
    base = own - place
    mine = pl.ds(pl.multiple_of(core * BLK, BLK), BLK)
    other = pl.ds(pl.multiple_of((1 - core) * BLK, BLK), BLK)
    x = chip % wide
    y = chip // wide
    earlier = jnp.minimum(reach, chip)

    def load(src, dst, n):
        return pltpu.make_async_copy(src, dst, load_sem.at[n])

    loads = [
        load(k_h, kv.at[0, 0, mine], 0),
        load(v_h, kv.at[0, 1, mine], 1),
        load(hid_h, hid, 2),
        load(down_h, down, 3),
        load(up_h, up, 4),
        load(rq_h, rq, 5),
        load(do_h, do, 6),
        load(db_h, db, 7),
        load(da_h, da, 8),
    ]
    loads[0].start()
    loads[1].start()
    barrier = pltpu.get_barrier_semaphore()
    partners = [(own, (m + step) % mp) for step in range(1, mp)]
    partners += [(base + (place + step) % span, m) for step in range(1, span)]
    partners += [((own + span * step) % seq, m) for step in range(1, seq // span)]
    for peer in partners:
        pl.semaphore_signal(barrier, inc=1, device_id=peer, device_id_type=MESH)
    for n in (7, 8, 2, 3, 6, 4, 5):
        loads[n].start()
    loads[0].wait()
    loads[1].wait()
    pl.semaphore_wait(barrier, len(partners))

    def exchange(buf, send, recv):
        copies = []
        for step in range(1, mp):
            peer = (m + step) % mp
            copies.append(
                pltpu.make_async_remote_copy(
                    src_ref=buf.at[m], dst_ref=buf.at[m],
                    send_sem=send.at[step], recv_sem=recv.at[step],
                    device_id=(own, peer), device_id_type=MESH,
                )
            )
        return copies

    def at_chip(to_x, to_y):
        return ((to_y * wide + to_x) * 2 + core, m)

    def column_copy(dy):
        return pltpu.make_async_remote_copy(
            src_ref=kv.at[0, :, mine], dst_ref=kv.at[dy * wide, :, mine],
            send_sem=col_send.at[dy], recv_sem=kv_recv.at[dy * wide],
            device_id=at_chip(x, y + dy), device_id_type=MESH,
        )

    def row_copy(dy, to_x):
        return pltpu.make_async_remote_copy(
            src_ref=kv.at[dy * wide, :, mine], dst_ref=kv.at[dy * wide + to_x - x, :, mine],
            send_sem=row_send.at[dy, to_x], recv_sem=kv_recv.at[dy * wide + to_x - x],
            device_id=at_chip(to_x, y), device_id_type=MESH,
        )

    def row_readers(dy, act):
        for to_x in range(wide):
            reads = (to_x > x, to_x != x, to_x < x)[dy]

            @pl.when(jnp.logical_and(y >= dy, reads))
            def _():
                act(row_copy(dy, to_x))

    def kv_land(e):
        return pltpu.make_async_remote_copy(
            src_ref=kv.at[0, :, mine], dst_ref=kv.at[e, :, mine],
            send_sem=col_send.at[0], recv_sem=kv_recv.at[e],
            device_id=(sib, m), device_id_type=MESH,
        )

    def forward(e):
        return pltpu.make_async_remote_copy(
            src_ref=kv.at[e, :, mine], dst_ref=kv.at[e, :, mine],
            send_sem=fwd_send.at[e], recv_sem=fwd_recv.at[e],
            device_id=(sib, m), device_id_type=MESH,
        )

    def forward_land(e):
        return pltpu.make_async_remote_copy(
            src_ref=kv.at[e, :, other], dst_ref=kv.at[e, :, other],
            send_sem=fwd_send.at[e], recv_sem=fwd_recv.at[e],
            device_id=(sib, m), device_id_type=MESH,
        )

    @pl.when(y + 1 < tall)
    def _():
        column_copy(1).start()

    forward(0).start()
    row_readers(0, lambda copy: copy.start())

    loads[7].wait()
    loads[8].wait()
    start = jnp.int32(0)
    first = jnp.int32(0)
    adapter = jnp.int32(0)
    bounds = []
    for d in range(docs):
        end = start + db[d]
        inside = jnp.logical_and(own >= start, own < end)
        first = jnp.where(inside, start, first)
        adapter = jnp.where(inside, da[d], adapter)
        bounds.append((start, end, da[d]))
        start = end

    loads[2].wait()
    loads[3].wait()
    lowx[m] = dot_nt(down[adapter], hid[...])
    low_copies = exchange(lowx, low_send, low_recv)
    for one in low_copies:
        one.start()

    @pl.when(y + 1 < tall)
    def _():
        column_copy(1).wait_send()

    @pl.when(y + 2 < tall)
    def _():
        column_copy(2).start()

    loads[6].wait()
    for h in range(heads):
        here = slice(h * BLK, (h + 1) * BLK)
        part = do[:, h * HEAD : (h + 1) * HEAD]
        dos[here, :] = part
        dot_t[:, here] = part.T

    size = select.shape
    row = lax.broadcasted_iota(jnp.int32, size, 0)
    col = lax.broadcasted_iota(jnp.int32, size, 1)
    same = (row % RANK) == (col % RANK)
    row_a = row // RANK
    col_s = base + col // RANK
    hit = jnp.zeros(size, F32)
    for begin, end, name in bounds:
        inside = jnp.logical_and(col_s >= begin, col_s < end)
        inside = jnp.logical_and(inside, row_a == name)
        hit = jnp.where(jnp.logical_and(inside, same), 1.0, hit)
    select[...] = hit.astype(BF16)

    @pl.loop(earlier + 1, units)
    def _(e):
        sbuf[e] = jnp.full(sbuf.shape[1:], NEG, F32)
        dpbuf[e] = jnp.zeros(dpbuf.shape[1:], F32)
        kv[e] = jnp.zeros(kv.shape[1:], BF16)

    for dy in range(1, 3):

        @pl.when(y >= dy)
        def _():
            kv_land(dy * wide).wait_recv()
            forward(dy * wide).start()

        row_readers(dy, lambda copy: copy.start())

    @pl.loop(1, x + 1)
    def _(e):
        kv_land(e).wait_recv()
        forward(e).start()

    loads[4].wait()
    loads[5].wait()
    up_rows = up[adapter]
    for one in low_copies:
        one.wait_recv()
    low_sum = lowx[0]
    for step in range(1, mp):
        low_sum = low_sum + lowx[step]
    low_t = low_sum.astype(BF16)
    low = low_sum.T.astype(BF16)
    for h in range(heads):
        part = slice(h * HEAD, (h + 1) * HEAD)
        here = slice(h * BLK, (h + 1) * BLK)
        q = (rq[:, part].astype(F32) + dot(low, up_rows[:, part])).astype(BF16)
        qs[here, :] = q
        qt[:, here] = q.T

    u_rows = lax.broadcasted_iota(jnp.int32, (2 * BLK, CHUNK), 0)
    t_cols = lax.broadcasted_iota(jnp.int32, (2 * BLK, CHUNK), 1) % BLK

    def score_unit(e, diagonal):
        low_edge = (first - 2 * (chip - e)) * BLK
        keys = kv[e, 0]
        values = kv[e, 1]
        for at in range(0, cols, CHUNK):
            part = slice(at, at + CHUNK)
            s = dot(keys, qt[:, part])
            keep = u_rows >= low_edge
            if diagonal:
                keep = jnp.logical_and(keep, u_rows <= core * BLK + t_cols)
            s = jnp.where(keep, s, NEG)
            sbuf[e, :, part] = s
            dp = dot(values, dot_t[:, part])
            dpbuf[e, :, part] = dp
            top = jnp.max(s, axis=0, keepdims=True)
            if not diagonal:
                was = stat[0:1, part]
                top = jnp.maximum(top, was)
            p = jnp.exp2(s * fold - top * fold)
            total = jnp.sum(p, axis=0, keepdims=True)
            delta = jnp.sum(p * dp, axis=0, keepdims=True)
            if not diagonal:
                shrink = jnp.exp2((was - top) * fold)
                total = total + shrink * stat[8:9, part]
                delta = delta + shrink * stat[16:17, part]
            stat[0:1, part] = top
            stat[8:9, part] = total
            stat[16:17, part] = delta

    forward_land(0).wait_recv()
    score_unit(0, True)

    for dy in range(1, 3):

        @pl.when(y >= dy)
        def _():
            forward_land(dy * wide).wait_recv()
            score_unit(dy * wide, False)

    @pl.loop(1, earlier + 1 + LAG)
    def _(e):
        @pl.when(jnp.logical_and(jnp.logical_and(e > x, e <= earlier), e % wide != 0))
        def _():
            kv_land(e).wait_recv()
            forward(e).start()

        @pl.when(jnp.logical_and(e > LAG, (e - LAG) % wide != 0))
        def _():
            forward_land(e - LAG).wait_recv()
            score_unit(e - LAG, False)

    total = stat[8:9, :]
    stat[24:25, :] = stat[0:1, :] * fold + jnp.log(total) * LOG2E
    stat[16:17, :] = stat[16:17, :] / total
    for e in range(units):
        here = slice(e * 2 * BLK, (e + 1) * 2 * BLK)
        keys_t[:, here] = kv[e, 0].T
        vals_t[:, here] = kv[e, 1].T
        for at in range(0, cols, NARROW):
            part = slice(at, at + NARROW)
            p = jnp.exp2(sbuf[e, :, part] * fold - stat[24:25, part])
            dsbuf[here, part] = (p * (dpbuf[e, :, part] - stat[16:17, part])).astype(BF16)
            pbuf[here, part] = p.astype(BF16)
    dq_t = dot(keys_t[...], dsbuf[...]) * scale
    for h in range(heads):
        part = slice(h * HEAD, (h + 1) * HEAD)
        gqv[:, part] = dq_t[:, part].T.astype(BF16)

    dlowx[m] = dot_nt(up_rows, gqv[...])
    dlow_copies = exchange(dlowx, dlow_send, dlow_recv)
    for one in dlow_copies:
        one.start()
    gq_copy = pltpu.make_async_copy(gqv, gq_h, out_sem.at[1])
    gq_copy.start()

    own16 = pl.ds(pl.multiple_of(own * RANK, RANK), RANK)
    place16 = pl.ds(pl.multiple_of(place * RANK, RANK), RANK)
    rest1 = pl.ds(0, (span - 1) * RANK)
    rest2 = pl.ds(0, (seq - 1) * RANK)

    def spread(kind, product):
        for t in range(span):
            piece[kind, t] = product[:, t * 128 : (t + 1) * 128].astype(BF16)

        @pl.loop(1, span)
        def _(step):
            peer = (place + step) % span
            pltpu.make_async_remote_copy(
                src_ref=piece.at[kind, peer], dst_ref=got.at[kind, place16],
                send_sem=a1_send.at[kind], recv_sem=a1_recv.at[kind],
                device_id=(base + peer, m), device_id_type=MESH,
            ).start()

    def settle(kind):
        land = got.at[kind, rest1]
        pltpu.make_async_copy(land, land, a1_recv.at[kind]).wait()
        got[kind, place16, :] = piece[kind, place]
        red[kind] = dot(select[...], got[kind]).astype(BF16)

        @pl.loop(1, seq)
        def _(step):
            peer = (own + step) % seq
            pltpu.make_async_remote_copy(
                src_ref=red.at[kind, pl.ds(pl.multiple_of(peer * RANK, RANK), RANK)],
                dst_ref=fin.at[kind, own16],
                send_sem=a2_send.at[kind], recv_sem=a2_recv.at[kind],
                device_id=(peer, m), device_id_type=MESH,
            ).start()

    def finish(kind):
        land = fin.at[kind, rest2]
        pltpu.make_async_copy(land, land, a2_recv.at[kind]).wait()
        fin[kind, own16, :] = red[kind, own16, :]
        for t in range(span):
            whole = jnp.zeros((RANK, 128), F32)
            for line in range(seq // span):
                at = (line * span + t) * RANK
                whole = whole + fin[kind, at : at + RANK, :].astype(F32)
            gout[kind, :, t * 128 : (t + 1) * 128] = whole

    def sib_copy(g):
        return pltpu.make_async_remote_copy(
            src_ref=sib_out.at[g], dst_ref=sib_in.at[g],
            send_sem=sib_send.at[g], recv_sem=sib_recv.at[g],
            device_id=(sib, m), device_id_type=MESH,
        )

    def merge_copy(e):
        owner = chip - e
        to_x = owner % wide
        dy = y - owner // wide
        return to_x, pltpu.make_async_remote_copy(
            src_ref=dkv_out.at[e], dst_ref=dkv_in.at[dy, x],
            send_sem=dkv_send.at[e], recv_sem=dkv_recv.at[dy, x],
            device_id=at_chip(to_x, y), device_id_type=MESH,
        )

    def merge_land(dy, from_x):
        return pltpu.make_async_remote_copy(
            src_ref=dkv_out.at[0], dst_ref=dkv_in.at[dy, from_x],
            send_sem=dkv_send.at[0], recv_sem=dkv_recv.at[dy, from_x],
            device_id=(sib, m), device_id_type=MESH,
        )

    def home_copy(dy):
        return pltpu.make_async_remote_copy(
            src_ref=home_out.at[dy], dst_ref=home_in.at[dy],
            send_sem=home_send.at[dy], recv_sem=home_recv.at[dy],
            device_id=at_chip(x, y - dy), device_id_type=MESH,
        )

    def merge_row(dy):
        for from_x in range(wide):
            writes = (from_x > x, from_x != x, from_x < x)[dy]

            @pl.when(jnp.logical_and(y >= dy, writes))
            def _():
                merge_land(dy, from_x).wait_recv()
                total_kv[dy] = total_kv[dy] + dkv_in[dy, from_x].astype(F32)

    def weigh(g):
        here = slice(g * GROUP * 2 * BLK, (g + 1) * GROUP * 2 * BLK)
        pair[0] = dot(dsbuf[here, :], qs[...]) * scale
        pair[1] = dot(pbuf[here, :], dos[...])
        for k in range(GROUP):
            for kind in range(2):
                lower = pl.ds(pl.multiple_of((2 * k + core) * BLK, BLK), BLK)
                upper = pl.ds(pl.multiple_of((2 * k + 1 - core) * BLK, BLK), BLK)
                own_st[g, k, kind] = pair[kind, lower, :]
                sib_out[g, k, kind] = pair[kind, upper, :].astype(BF16)
        sib_copy(g).start()

    def pass_on(g):
        sib_copy(g).wait_recv()
        for k in range(GROUP - 1, -1, -1):
            e = g * GROUP + k
            merged = own_st[g, k] + sib_in[g, k].astype(F32)
            if e % wide == 0:
                total_kv[e // wide] = merged
            else:
                dkv_out[e] = merged.astype(BF16)
                to_x, copy = merge_copy(e)

                @pl.when(e <= earlier)
                def _():
                    copy.start()

    spread(0, dot(low_t, gqv[...]))
    for g in range(groups - 1, -1, -1):
        weigh(g)
        if g < groups - 1:
            pass_on(g + 1)

    for one in dlow_copies:
        one.wait_recv()
    dlow_sum = dlowx[0]
    for step in range(1, mp):
        dlow_sum = dlow_sum + dlowx[step]
    spread(1, dot(dlow_sum.astype(BF16), hid[...]))
    pass_on(0)
    settle(0)

    out_t = dot(vals_t[...], pbuf[...])
    for h in range(heads):
        part = slice(h * HEAD, (h + 1) * HEAD)
        outv[:, part] = out_t[:, part].T.astype(BF16)
    out_copy = pltpu.make_async_copy(outv, out_h, out_sem.at[0])
    out_copy.start()

    def send_home(dy):
        merge_row(dy)

        @pl.when(y >= dy)
        def _():
            home_out[dy] = total_kv[dy].astype(BF16)
            home_copy(dy).start()

    send_home(2)
    settle(1)
    send_home(1)
    merge_row(0)
    finish(0)
    gb_copy = pltpu.make_async_copy(gout.at[0], gb_h.at[0], out_sem.at[4])
    gb_copy.start()
    for dy in range(1, 3):

        @pl.when(y + dy < tall)
        def _():
            home_copy(dy).wait_recv()
            total_kv[0] = total_kv[0] + home_in[dy].astype(F32)

    gkv[...] = total_kv[0].astype(BF16)
    gk_copy = pltpu.make_async_copy(gkv.at[0], gk_h, out_sem.at[2])
    gv_copy = pltpu.make_async_copy(gkv.at[1], gv_h, out_sem.at[3])
    gk_copy.start()
    gv_copy.start()

    finish(1)
    ga_copy = pltpu.make_async_copy(gout.at[1], ga_h.at[0], out_sem.at[5])
    ga_copy.start()

    for one in low_copies + dlow_copies:
        one.wait_send()

    for dy in range(3):
        row_readers(dy, lambda copy: copy.wait_send())
    for dy in range(1, 3):

        @pl.when(y >= dy)
        def _():
            home_copy(dy).wait_send()

    @pl.when(y + 2 < tall)
    def _():
        column_copy(2).wait_send()

    @pl.loop(0, earlier + 1)
    def _(e):
        forward(e).wait_send()

    for g in range(groups):
        sib_copy(g).wait_send()
    for e in range(units):
        if e % wide:
            to_x, copy = merge_copy(e)

            @pl.when(e <= earlier)
            def _():
                copy.wait_send()

    for kind in range(2):
        sent = got.at[kind, rest1]
        pltpu.make_async_copy(sent, sent, a1_send.at[kind]).wait()
        sent = red.at[kind, rest2]
        pltpu.make_async_copy(sent, sent, a2_send.at[kind]).wait()
    for one in (out_copy, gq_copy, gk_copy, gv_copy, ga_copy, gb_copy):
        one.wait()


def place_kernel(count, *refs):
    sources, targets, held = refs[:count], refs[count : 2 * count], refs[2 * count : 3 * count]
    in_sem, out_sem = refs[3 * count :]
    ins = [pltpu.make_async_copy(sources[n], held[n], in_sem.at[n]) for n in range(count)]
    outs = [pltpu.make_async_copy(held[n], targets[n], out_sem.at[n]) for n in range(count)]
    for one in ins:
        one.start()
    for came, goes in zip(ins, outs):
        came.wait()
        goes.start()
    for one in outs:
        one.wait()


def on_device(
    hidden_rows, rotated_queries, rotated_keys, value_rows, adapter_down, adapter_up,
    output_gradient, document_blocks, document_adapter,
):
    seq = lax.axis_size("seq")
    mp = lax.axis_size("mp")
    rows, cols = hidden_rows.shape
    adapters = adapter_down.shape[0]
    units = seq // 4 + 1
    wide = seq // 8
    span = cols // 128
    groups = units // GROUP
    docs = document_blocks.shape[0]
    any_space = pl.BlockSpec(memory_space=pl.ANY)
    dma = pltpu.SemaphoreType.DMA
    vmem = pltpu.VMEM
    shapes = (
        jax.ShapeDtypeStruct((rows, cols), BF16),
        jax.ShapeDtypeStruct((rows, cols), BF16),
        jax.ShapeDtypeStruct((rows, HEAD), BF16),
        jax.ShapeDtypeStruct((rows, HEAD), BF16),
        jax.ShapeDtypeStruct((1, RANK, cols), F32),
        jax.ShapeDtypeStruct((1, RANK, cols), F32),
    )
    made = pl.pallas_call(
        functools.partial(kernel, seq, mp, docs),
        out_shape=shapes,
        in_specs=[any_space] * 9,
        out_specs=[any_space] * 6,
        scratch_shapes=[
            pltpu.SMEM((docs,), jnp.int32),
            pltpu.SMEM((docs,), jnp.int32),
            vmem((rows, cols), BF16),
            vmem((rows, cols), BF16),
            vmem((adapters, RANK, cols), BF16),
            vmem((adapters, RANK, cols), BF16),
            vmem((rows, cols), BF16),
            vmem((units, 2, 2 * BLK, HEAD), BF16),
            vmem((cols, HEAD), BF16),
            vmem((HEAD, cols), BF16),
            vmem((cols, HEAD), BF16),
            vmem((HEAD, cols), BF16),
            vmem((units, 2 * BLK, cols), F32),
            vmem((units, 2 * BLK, cols), F32),
            vmem((units * 2 * BLK, cols), BF16),
            vmem((units * 2 * BLK, cols), BF16),
            vmem((mp, RANK, rows), F32),
            vmem((mp, RANK, rows), F32),
            vmem((32, cols), F32),
            vmem((HEAD, units * 2 * BLK), BF16),
            vmem((HEAD, units * 2 * BLK), BF16),
            vmem((rows, cols), BF16),
            vmem((rows, cols), BF16),
            vmem((2, GROUP * 2 * BLK, HEAD), F32),
            vmem((groups, GROUP, 2, BLK, HEAD), F32),
            vmem((groups, GROUP, 2, BLK, HEAD), BF16),
            vmem((groups, GROUP, 2, BLK, HEAD), BF16),
            vmem((units, 2, BLK, HEAD), BF16),
            vmem((3, wide, 2, BLK, HEAD), BF16),
            vmem((3, 2, BLK, HEAD), BF16),
            vmem((3, 2, BLK, HEAD), BF16),
            vmem((2, BLK, HEAD), BF16),
            vmem((3, 2, BLK, HEAD), F32),
            vmem((adapters * RANK, span * RANK), BF16),
            vmem((2, span, RANK, 128), BF16),
            vmem((2, span * RANK, 128), BF16),
            vmem((2, seq * RANK, 128), BF16),
            vmem((2, seq * RANK, 128), BF16),
            vmem((2, RANK, cols), F32),
            dma((9,)), dma((6,)),
            dma((mp,)), dma((mp,)), dma((mp,)), dma((mp,)),
            dma((3,)), dma((3, wide)), dma((units,)), dma((units,)), dma((units,)),
            dma((groups,)), dma((groups,)), dma((units,)), dma((3, wide)),
            dma((3,)), dma((3,)),
            dma((2,)), dma((2,)), dma((2,)), dma((2,)),
        ],
        compiler_params=pltpu.CompilerParams(
            collective_id=0, has_side_effects=True, vmem_limit_bytes=63 * 1024 * 1024
        ),
    )(
        document_blocks, document_adapter, hidden_rows, rotated_queries, rotated_keys,
        value_rows, adapter_down, adapter_up, output_gradient,
    )
    return pl.pallas_call(
        functools.partial(place_kernel, len(shapes)),
        out_shape=shapes,
        in_specs=[any_space] * len(shapes),
        out_specs=[any_space] * len(shapes),
        scratch_shapes=[vmem(one.shape, one.dtype) for one in shapes]
        + [dma((len(shapes),)), dma((len(shapes),))],
    )(*made)


def solution(mesh):
    return jax.shard_map(
        on_device,
        mesh=mesh,
        in_specs=(
            P("seq", "mp"),
            P("seq", "mp"),
            P("seq", "mp"),
            P("seq", "mp"),
            P(None, None, "mp"),
            P(None, None, "mp"),
            P("seq", "mp"),
            P(),
            P(),
        ),
        out_specs=(
            P("seq", "mp"),
            P("seq", "mp"),
            P("seq", "mp"),
            P("seq", "mp"),
            P("seq", None, "mp"),
            P("seq", None, "mp"),
        ),
        check_vma=False,
    )
```

```python
import functools
import math

import jax
import jax.numpy as jnp
from jax import lax
from jax.experimental import pallas as pl
from jax.experimental.pallas import tpu as pltpu
from jax.sharding import PartitionSpec as P

HEAD = 128
BLK = 128
RANK = 16
CHUNK = 1024
NARROW = 256
GROUP = 3
LAG = 3
NEG = -1e30
LOG2E = 1.4426950408889634
MESH = pl.DeviceIdType.MESH
F32 = jnp.float32
BF16 = jnp.bfloat16

NT = (((1,), (1,)), ((), ()))


def dot(a, b):
    return jnp.dot(a, b, preferred_element_type=F32)


def dot_nt(a, b):
    return lax.dot_general(a, b, NT, preferred_element_type=F32)


def kernel(
    seq, mp, docs,
    db_h, da_h, hid_h, rq_h, k_h, v_h, down_h, up_h, do_h,
    outv, gqv, gk, gv, ga, gb,
    db, da, hid, rq, down, up, do, kv, qs, qt, dos, dot_t, sbuf, dpbuf, pbuf, dsbuf,
    lowx, dlowx, stat, keys_t, vals_t, pair, own_st, sib_out, sib_in,
    dkv_out, dkv_in, home_out, home_in, total_kv, select, piece, got, red, fin,
    load_sem,
    low_send, low_recv, dlow_send, dlow_recv,
    col_send, row_send, direct_send, kv_recv, fwd_send, fwd_recv, sib_send, sib_recv, dkv_send, dkv_recv,
    home_send, home_recv,
    a1_send, a1_recv, a2_send, a2_recv,
):
    reach = seq // 4
    chips = seq // 2
    units = reach + 1
    wide = reach // 2
    tall = chips // wide
    cols = hid.shape[1]
    heads = cols // HEAD
    span = cols // 128
    groups = units // GROUP
    scale = 1.0 / math.sqrt(HEAD)
    fold = scale * LOG2E

    own = lax.axis_index("seq")
    m = lax.axis_index("mp")
    chip = own // 2
    core = own % 2
    sib = own + 1 - 2 * core
    place = own % span
    base = own - place
    mine = pl.ds(pl.multiple_of(core * BLK, BLK), BLK)
    other = pl.ds(pl.multiple_of((1 - core) * BLK, BLK), BLK)
    x = chip % wide
    y = chip // wide
    earlier = jnp.minimum(reach, chip)

    def at_chip(to_x, to_y):
        return ((to_y * wide + to_x) * 2 + core, m)

    def load(src, dst, n):
        return pltpu.make_async_copy(src, dst, load_sem.at[n])

    loads = [
        load(k_h, kv.at[0, 0, mine], 0),
        load(v_h, kv.at[0, 1, mine], 1),
        load(hid_h, hid, 2),
        load(down_h, down, 3),
        load(up_h, up, 4),
        load(rq_h, rq, 5),
        load(do_h, do, 6),
        load(db_h, db, 7),
        load(da_h, da, 8),
    ]
    loads[0].start()
    loads[1].start()
    barrier = pltpu.get_barrier_semaphore()
    partners = [(own, (m + step) % mp) for step in range(1, mp)]
    partners += [(base + (place + step) % span, m) for step in range(1, span)]
    partners += [((own + span * step) % seq, m) for step in range(1, seq // span)]
    for peer in partners:
        pl.semaphore_signal(barrier, inc=1, device_id=peer, device_id_type=MESH)
    skips = wide - 1
    greeted = len(partners)
    if skips:
        greeted += jnp.where(x == skips, jnp.minimum(2, tall - 1 - y), 0)
        for dy in range(1, 3):

            @pl.when(jnp.logical_and(x == 0, y >= dy))
            def _():
                pl.semaphore_signal(
                    barrier, inc=1, device_id=at_chip(skips, y - dy), device_id_type=MESH
                )

    for n in (7, 8, 2, 3, 6, 4, 5):
        loads[n].start()
    loads[0].wait()
    loads[1].wait()
    pl.semaphore_wait(barrier, greeted)

    def exchange(buf, send, recv):
        copies = []
        for step in sorted(range(1, mp), key=lambda step: abs(step - mp // 2)):
            peer = (m + step) % mp
            copies.append(
                pltpu.make_async_remote_copy(
                    src_ref=buf.at[m], dst_ref=buf.at[m],
                    send_sem=send.at[step], recv_sem=recv.at[step],
                    device_id=(own, peer), device_id_type=MESH,
                )
            )
        return copies

    def column_copy(dy):
        return pltpu.make_async_remote_copy(
            src_ref=kv.at[0, :, mine], dst_ref=kv.at[dy * wide, :, mine],
            send_sem=col_send.at[dy], recv_sem=kv_recv.at[dy * wide],
            device_id=at_chip(x, y + dy), device_id_type=MESH,
        )

    def direct_copy(dy):
        e = dy * wide - skips
        return pltpu.make_async_remote_copy(
            src_ref=kv.at[0, :, mine], dst_ref=kv.at[e, :, mine],
            send_sem=direct_send.at[dy], recv_sem=kv_recv.at[e],
            device_id=at_chip(0, y + dy), device_id_type=MESH,
        )

    def direct(dy, act):
        if skips:

            @pl.when(jnp.logical_and(x == skips, y + dy < tall))
            def _():
                act(direct_copy(dy))

    def row_copy(dy, to_x):
        return pltpu.make_async_remote_copy(
            src_ref=kv.at[dy * wide, :, mine], dst_ref=kv.at[dy * wide + to_x - x, :, mine],
            send_sem=row_send.at[dy, to_x], recv_sem=kv_recv.at[dy * wide + to_x - x],
            device_id=at_chip(to_x, y), device_id_type=MESH,
        )

    def row_readers(dy, act):
        for to_x in range(wide):
            reads = (to_x > x, to_x != x, to_x < x)[dy]
            if dy and to_x == 0:
                reads = jnp.logical_and(reads, x != skips)

            @pl.when(jnp.logical_and(y >= dy, reads))
            def _():
                act(row_copy(dy, to_x))

    def kv_land(e):
        return pltpu.make_async_remote_copy(
            src_ref=kv.at[0, :, mine], dst_ref=kv.at[e, :, mine],
            send_sem=col_send.at[0], recv_sem=kv_recv.at[e],
            device_id=(sib, m), device_id_type=MESH,
        )

    def forward(e):
        return pltpu.make_async_remote_copy(
            src_ref=kv.at[e, :, mine], dst_ref=kv.at[e, :, mine],
            send_sem=fwd_send.at[e], recv_sem=fwd_recv.at[e],
            device_id=(sib, m), device_id_type=MESH,
        )

    def forward_land(e):
        return pltpu.make_async_remote_copy(
            src_ref=kv.at[e, :, other], dst_ref=kv.at[e, :, other],
            send_sem=fwd_send.at[e], recv_sem=fwd_recv.at[e],
            device_id=(sib, m), device_id_type=MESH,
        )

    @pl.when(y + 1 < tall)
    def _():
        column_copy(1).start()

    forward(0).start()
    row_readers(0, lambda copy: copy.start())

    loads[7].wait()
    loads[8].wait()
    start = jnp.int32(0)
    first = jnp.int32(0)
    adapter = jnp.int32(0)
    bounds = []
    for d in range(docs):
        end = start + db[d]
        inside = jnp.logical_and(own >= start, own < end)
        first = jnp.where(inside, start, first)
        adapter = jnp.where(inside, da[d], adapter)
        bounds.append((start, end, da[d]))
        start = end

    loads[2].wait()
    loads[3].wait()
    lowx[m] = dot_nt(down[adapter], hid[...])
    low_copies = exchange(lowx, low_send, low_recv)
    for one in low_copies:
        one.start()

    @pl.when(y + 1 < tall)
    def _():
        column_copy(1).wait_send()

    @pl.when(y + 2 < tall)
    def _():
        column_copy(2).start()

    for dy in range(1, 3):
        direct(dy, lambda copy: copy.start())
    loads[6].wait()
    for h in range(heads):
        here = slice(h * BLK, (h + 1) * BLK)
        part = do[:, h * HEAD : (h + 1) * HEAD]
        dos[here, :] = part
        dot_t[:, here] = part.T

    size = select.shape
    row = lax.broadcasted_iota(jnp.int32, size, 0)
    col = lax.broadcasted_iota(jnp.int32, size, 1)
    same = (row % RANK) == (col % RANK)
    row_a = row // RANK
    col_s = base + col // RANK
    hit = jnp.zeros(size, F32)
    for begin, end, name in bounds:
        inside = jnp.logical_and(col_s >= begin, col_s < end)
        inside = jnp.logical_and(inside, row_a == name)
        hit = jnp.where(jnp.logical_and(inside, same), 1.0, hit)
    select[...] = hit.astype(BF16)

    @pl.loop(earlier + 1, units)
    def _(e):
        sbuf[e] = jnp.full(sbuf.shape[1:], NEG, F32)
        dpbuf[e] = jnp.zeros(dpbuf.shape[1:], F32)
        keys_t[e] = jnp.zeros(keys_t.shape[1:], BF16)
        vals_t[e] = jnp.zeros(vals_t.shape[1:], BF16)

    for dy in range(1, 3):

        @pl.when(y >= dy)
        def _():
            kv_land(dy * wide).wait_recv()
            forward(dy * wide).start()

        row_readers(dy, lambda copy: copy.start())

    @pl.loop(1, x + 1)
    def _(e):
        kv_land(e).wait_recv()
        forward(e).start()

    loads[4].wait()
    loads[5].wait()
    up_rows = up[adapter]
    for one in low_copies:
        one.wait_recv()
    low_sum = lowx[0]
    for step in range(1, mp):
        low_sum = low_sum + lowx[step]
    low_t = low_sum.astype(BF16)
    low = low_sum.T.astype(BF16)
    for h in range(heads):
        part = slice(h * HEAD, (h + 1) * HEAD)
        here = slice(h * BLK, (h + 1) * BLK)
        q = (rq[:, part].astype(F32) + dot(low, up_rows[:, part])).astype(BF16)
        qs[here, :] = q
        qt[:, here] = q.T

    u_rows = lax.broadcasted_iota(jnp.int32, (2 * BLK, CHUNK), 0)
    t_cols = lax.broadcasted_iota(jnp.int32, (2 * BLK, CHUNK), 1) % BLK

    def score_unit(e, diagonal):
        low_edge = (first - 2 * (chip - e)) * BLK
        keys = kv[e, 0]
        values = kv[e, 1]
        keys_t[e] = keys.T
        vals_t[e] = values.T
        for at in range(0, cols, CHUNK):
            part = slice(at, at + CHUNK)
            s = dot(keys, qt[:, part])
            keep = u_rows >= low_edge
            if diagonal:
                keep = jnp.logical_and(keep, u_rows <= core * BLK + t_cols)
            s = jnp.where(keep, s, NEG)
            sbuf[e, :, part] = s
            dp = dot(values, dot_t[:, part])
            dpbuf[e, :, part] = dp
            top = jnp.max(s, axis=0, keepdims=True)
            if not diagonal:
                was = stat[0:1, part]
                top = jnp.maximum(top, was)
            p = jnp.exp2(s * fold - top * fold)
            total = jnp.sum(p, axis=0, keepdims=True)
            delta = jnp.sum(p * dp, axis=0, keepdims=True)
            if not diagonal:
                shrink = jnp.exp2((was - top) * fold)
                total = total + shrink * stat[8:9, part]
                delta = delta + shrink * stat[16:17, part]
            stat[0:1, part] = top
            stat[8:9, part] = total
            stat[16:17, part] = delta

    forward_land(0).wait_recv()
    score_unit(0, True)

    for dy in range(1, 3):

        @pl.when(y >= dy)
        def _():
            forward_land(dy * wide).wait_recv()
            score_unit(dy * wide, False)

    @pl.loop(1, earlier + 1 + LAG)
    def _(e):
        @pl.when(jnp.logical_and(jnp.logical_and(e > x, e <= earlier), e % wide != 0))
        def _():
            kv_land(e).wait_recv()
            forward(e).start()

        @pl.when(jnp.logical_and(e > LAG, (e - LAG) % wide != 0))
        def _():
            forward_land(e - LAG).wait_recv()
            score_unit(e - LAG, False)

    total = stat[8:9, :]
    stat[24:25, :] = stat[0:1, :] * fold + jnp.log(total) * LOG2E
    stat[16:17, :] = stat[16:17, :] / total
    for e in range(units):
        here = slice(e * 2 * BLK, (e + 1) * 2 * BLK)
        for at in range(0, cols, NARROW):
            part = slice(at, at + NARROW)
            p = jnp.exp2(sbuf[e, :, part] * fold - stat[24:25, part])
            dsbuf[here, part] = (p * (dpbuf[e, :, part] - stat[16:17, part])).astype(BF16)
            pbuf[here, part] = p.astype(BF16)
    def all_units(turned):
        return jnp.concatenate([turned[e] for e in range(units)], axis=1)

    dq_t = dot(all_units(keys_t), dsbuf[...]) * scale
    for h in range(heads):
        part = slice(h * HEAD, (h + 1) * HEAD)
        gqv[:, part] = dq_t[:, h * BLK : (h + 1) * BLK].T.astype(BF16)
    dlowx[m] = dot_nt(up_rows, gqv[...])
    dlow_copies = exchange(dlowx, dlow_send, dlow_recv)
    for one in dlow_copies:
        one.start()

    own16 = pl.ds(pl.multiple_of(own * RANK, RANK), RANK)
    place16 = pl.ds(pl.multiple_of(place * RANK, RANK), RANK)
    rest1 = pl.ds(0, (span - 1) * RANK)
    rest2 = pl.ds(0, (seq - 1) * RANK)

    def spread(kind, product):
        for t in range(span):
            piece[kind, t] = product[:, t * 128 : (t + 1) * 128].astype(BF16)

        @pl.loop(1, span)
        def _(step):
            peer = (place + step) % span
            pltpu.make_async_remote_copy(
                src_ref=piece.at[kind, peer], dst_ref=got.at[kind, place16],
                send_sem=a1_send.at[kind], recv_sem=a1_recv.at[kind],
                device_id=(base + peer, m), device_id_type=MESH,
            ).start()

    def settle(kind):
        land = got.at[kind, rest1]
        pltpu.make_async_copy(land, land, a1_recv.at[kind]).wait()
        got[kind, place16, :] = piece[kind, place]
        red[kind] = dot(select[...], got[kind]).astype(BF16)

        @pl.loop(0, seq - 1)
        def _(step):
            peer = (own + 1 + (step + seq // 2 - 1) % (seq - 1)) % seq
            pltpu.make_async_remote_copy(
                src_ref=red.at[kind, pl.ds(pl.multiple_of(peer * RANK, RANK), RANK)],
                dst_ref=fin.at[kind, own16],
                send_sem=a2_send.at[kind], recv_sem=a2_recv.at[kind],
                device_id=(peer, m), device_id_type=MESH,
            ).start()

    def finish(kind):
        land = fin.at[kind, rest2]
        pltpu.make_async_copy(land, land, a2_recv.at[kind]).wait()
        fin[kind, own16, :] = red[kind, own16, :]
        for t in range(span):
            whole = jnp.zeros((RANK, 128), F32)
            for line in range(seq // span):
                at = (line * span + t) * RANK
                whole = whole + fin[kind, at : at + RANK, :].astype(F32)
            (gb, ga)[kind][0, :, t * 128 : (t + 1) * 128] = whole

    def sib_copy(g):
        return pltpu.make_async_remote_copy(
            src_ref=sib_out.at[g], dst_ref=sib_in.at[g],
            send_sem=sib_send.at[g], recv_sem=sib_recv.at[g],
            device_id=(sib, m), device_id_type=MESH,
        )

    def merge_copy(e):
        owner = chip - e
        to_x = owner % wide
        dy = y - owner // wide
        return to_x, pltpu.make_async_remote_copy(
            src_ref=dkv_out.at[e], dst_ref=dkv_in.at[dy, x],
            send_sem=dkv_send.at[e], recv_sem=dkv_recv.at[dy, x],
            device_id=at_chip(to_x, y), device_id_type=MESH,
        )

    def merge_land(dy, from_x):
        return pltpu.make_async_remote_copy(
            src_ref=dkv_out.at[0], dst_ref=dkv_in.at[dy, from_x],
            send_sem=dkv_send.at[0], recv_sem=dkv_recv.at[dy, from_x],
            device_id=(sib, m), device_id_type=MESH,
        )

    def home_copy(dy):
        return pltpu.make_async_remote_copy(
            src_ref=home_out.at[dy], dst_ref=home_in.at[dy],
            send_sem=home_send.at[dy], recv_sem=home_recv.at[dy],
            device_id=at_chip(x, y - dy), device_id_type=MESH,
        )

    def merge_row(dy):
        for from_x in range(wide):
            writes = (from_x > x, from_x != x, from_x < x)[dy]

            @pl.when(jnp.logical_and(y >= dy, writes))
            def _():
                merge_land(dy, from_x).wait_recv()
                total_kv[dy] = total_kv[dy] + dkv_in[dy, from_x].astype(F32)

    def weigh(g):
        here = slice(g * GROUP * 2 * BLK, (g + 1) * GROUP * 2 * BLK)
        pair[0] = dot(dsbuf[here, :], qs[...]) * scale
        pair[1] = dot(pbuf[here, :], dos[...])
        for k in range(GROUP):
            for kind in range(2):
                lower = pl.ds(pl.multiple_of((2 * k + core) * BLK, BLK), BLK)
                upper = pl.ds(pl.multiple_of((2 * k + 1 - core) * BLK, BLK), BLK)
                own_st[g, k, kind] = pair[kind, lower, :]
                sib_out[g, k, kind] = pair[kind, upper, :].astype(BF16)
        sib_copy(g).start()

    def pass_on(g):
        sib_copy(g).wait_recv()
        for k in range(GROUP - 1, -1, -1):
            e = g * GROUP + k
            merged = own_st[g, k] + sib_in[g, k].astype(F32)
            if e % wide == 0:
                total_kv[e // wide] = merged
            else:
                dkv_out[e] = merged.astype(BF16)
                to_x, copy = merge_copy(e)

                @pl.when(e <= earlier)
                def _():
                    copy.start()

    spread(0, dot(low_t, gqv[...]))
    for g in range(groups - 1, -1, -1):
        weigh(g)
        if g < groups - 1:
            pass_on(g + 1)

    for one in dlow_copies:
        one.wait_recv()
    dlow_sum = dlowx[0]
    for step in range(1, mp):
        dlow_sum = dlow_sum + dlowx[step]
    spread(1, dot(dlow_sum.astype(BF16), hid[...]))
    pass_on(0)
    settle(0)

    out_t = dot(all_units(vals_t), pbuf[...])
    for h in range(heads):
        part = slice(h * HEAD, (h + 1) * HEAD)
        outv[:, part] = out_t[:, part].T.astype(BF16)

    def send_home(dy):
        merge_row(dy)

        @pl.when(y >= dy)
        def _():
            home_out[dy] = total_kv[dy].astype(BF16)
            home_copy(dy).start()

    send_home(2)
    settle(1)
    send_home(1)
    merge_row(0)
    finish(0)
    for dy in range(1, 3):

        @pl.when(y + dy < tall)
        def _():
            home_copy(dy).wait_recv()
            total_kv[0] = total_kv[0] + home_in[dy].astype(F32)

    gk[...] = total_kv[0, 0].astype(BF16)
    gv[...] = total_kv[0, 1].astype(BF16)

    finish(1)

    for one in low_copies + dlow_copies:
        one.wait_send()

    for dy in range(3):
        row_readers(dy, lambda copy: copy.wait_send())
    for dy in range(1, 3):

        @pl.when(y >= dy)
        def _():
            home_copy(dy).wait_send()

    @pl.when(y + 2 < tall)
    def _():
        column_copy(2).wait_send()

    for dy in range(1, 3):
        direct(dy, lambda copy: copy.wait_send())

    @pl.loop(0, earlier + 1)
    def _(e):
        forward(e).wait_send()

    for g in range(groups):
        sib_copy(g).wait_send()
    for e in range(units):
        if e % wide:
            to_x, copy = merge_copy(e)

            @pl.when(e <= earlier)
            def _():
                copy.wait_send()

    for kind in range(2):
        sent = got.at[kind, rest1]
        pltpu.make_async_copy(sent, sent, a1_send.at[kind]).wait()
        sent = red.at[kind, rest2]
        pltpu.make_async_copy(sent, sent, a2_send.at[kind]).wait()


def place_kernel(count, *refs):
    sems = refs[2 * count]
    copies = [
        pltpu.make_async_copy(refs[n], refs[count + n], sems.at[n]) for n in range(count)
    ]
    for one in copies:
        one.start()
    for one in copies:
        one.wait()


def on_device(
    hidden_rows, rotated_queries, rotated_keys, value_rows, adapter_down, adapter_up,
    output_gradient, document_blocks, document_adapter,
):
    seq = lax.axis_size("seq")
    mp = lax.axis_size("mp")
    rows, cols = hidden_rows.shape
    adapters = adapter_down.shape[0]
    units = seq // 4 + 1
    wide = seq // 8
    span = cols // 128
    groups = units // GROUP
    docs = document_blocks.shape[0]
    any_space = pl.BlockSpec(memory_space=pl.ANY)
    dma = pltpu.SemaphoreType.DMA
    vmem = pltpu.VMEM
    shapes = (
        jax.ShapeDtypeStruct((rows, cols), BF16),
        jax.ShapeDtypeStruct((rows, cols), BF16),
        jax.ShapeDtypeStruct((rows, HEAD), BF16),
        jax.ShapeDtypeStruct((rows, HEAD), BF16),
        jax.ShapeDtypeStruct((1, RANK, cols), F32),
        jax.ShapeDtypeStruct((1, RANK, cols), F32),
    )
    made = pl.pallas_call(
        functools.partial(kernel, seq, mp, docs),
        out_shape=[vmem(one.shape, one.dtype) for one in shapes],
        in_specs=[any_space] * 9,
        out_specs=[pl.BlockSpec(memory_space=pltpu.VMEM)] * 6,
        scratch_shapes=[
            pltpu.SMEM((docs,), jnp.int32),
            pltpu.SMEM((docs,), jnp.int32),
            vmem((rows, cols), BF16),
            vmem((rows, cols), BF16),
            vmem((adapters, RANK, cols), BF16),
            vmem((adapters, RANK, cols), BF16),
            vmem((rows, cols), BF16),
            vmem((units, 2, 2 * BLK, HEAD), BF16),
            vmem((cols, HEAD), BF16),
            vmem((HEAD, cols), BF16),
            vmem((cols, HEAD), BF16),
            vmem((HEAD, cols), BF16),
            vmem((units, 2 * BLK, cols), F32),
            vmem((units, 2 * BLK, cols), F32),
            vmem((units * 2 * BLK, cols), BF16),
            vmem((units * 2 * BLK, cols), BF16),
            vmem((mp, RANK, rows), F32),
            vmem((mp, RANK, rows), F32),
            vmem((32, cols), F32),
            vmem((units, HEAD, 2 * BLK), BF16),
            vmem((units, HEAD, 2 * BLK), BF16),
            vmem((2, GROUP * 2 * BLK, HEAD), F32),
            vmem((groups, GROUP, 2, BLK, HEAD), F32),
            vmem((groups, GROUP, 2, BLK, HEAD), BF16),
            vmem((groups, GROUP, 2, BLK, HEAD), BF16),
            vmem((units, 2, BLK, HEAD), BF16),
            vmem((3, wide, 2, BLK, HEAD), BF16),
            vmem((3, 2, BLK, HEAD), BF16),
            vmem((3, 2, BLK, HEAD), BF16),
            vmem((3, 2, BLK, HEAD), F32),
            vmem((adapters * RANK, span * RANK), BF16),
            vmem((2, span, RANK, 128), BF16),
            vmem((2, span * RANK, 128), BF16),
            vmem((2, seq * RANK, 128), BF16),
            vmem((2, seq * RANK, 128), BF16),
            dma((9,)),
            dma((mp,)), dma((mp,)), dma((mp,)), dma((mp,)),
            dma((3,)), dma((3, wide)), dma((3,)), dma((units,)), dma((units,)), dma((units,)),
            dma((groups,)), dma((groups,)), dma((units,)), dma((3, wide)),
            dma((3,)), dma((3,)),
            dma((2,)), dma((2,)), dma((2,)), dma((2,)),
        ],
        compiler_params=pltpu.CompilerParams(
            collective_id=0, has_side_effects=True, vmem_limit_bytes=48 * 1024 * 1024
        ),
    )(
        *(
            pltpu.with_memory_space_constraint(one, pltpu.HBM)
            for one in (
                document_blocks, document_adapter, hidden_rows, rotated_queries, rotated_keys,
                value_rows, adapter_down, adapter_up, output_gradient,
            )
        )
    )
    return pl.pallas_call(
        functools.partial(place_kernel, len(shapes)),
        out_shape=shapes,
        in_specs=[any_space] * len(shapes),
        out_specs=[any_space] * len(shapes),
        scratch_shapes=[dma((len(shapes),))],
    )(*(pltpu.with_memory_space_constraint(one, pltpu.VMEM) for one in made))


def solution(mesh):
    return jax.shard_map(
        on_device,
        mesh=mesh,
        in_specs=(
            P("seq", "mp"),
            P("seq", "mp"),
            P("seq", "mp"),
            P("seq", "mp"),
            P(None, None, "mp"),
            P(None, None, "mp"),
            P("seq", "mp"),
            P(),
            P(),
        ),
        out_specs=(
            P("seq", "mp"),
            P("seq", "mp"),
            P("seq", "mp"),
            P("seq", "mp"),
            P("seq", None, "mp"),
            P("seq", None, "mp"),
        ),
        check_vma=False,
    )
```

```python
import functools
import math

import jax
import jax.numpy as jnp
from jax import lax
from jax.experimental import pallas as pl
from jax.experimental.pallas import tpu as pltpu
from jax.sharding import PartitionSpec as P

HEAD = 128
BLK = 128
RANK = 16
NARROW = 256
GROUP = 3
NEG = -1e30
LOG2E = 1.4426950408889634
MESH = pl.DeviceIdType.MESH
F32 = jnp.float32
BF16 = jnp.bfloat16

NT = (((1,), (1,)), ((), ()))


def dot(a, b):
    return jnp.dot(a, b, preferred_element_type=F32)


def dot_nt(a, b):
    return lax.dot_general(a, b, NT, preferred_element_type=F32)


def kernel(
    seq, mp, docs,
    db_h, da_h, hid_h, rq_h, k_h, v_h, down_h, up_h, do_h,
    outv, gqv, gk, gv, ga, gb,
    db, da, hid, rq, down, up, do, kv, qs, qt, dos, dot_t, sbuf, dpbuf, pbuf, dsbuf,
    lowx, dlowx, stat, shifts, keys_t, vals_t, pair, own_st, sib_out, sib_in,
    dkv_out, dkv_in, home_out, home_in, total_kv, select, piece, got, red, fin,
    load_sem,
    low_send, low_recv, dlow_send, dlow_recv,
    col_send, row_send, direct_send, kv_recv, fwd_send, fwd_recv, sib_send, sib_recv, dkv_send, dkv_recv,
    home_send, home_recv,
    a1_send, a1_recv, a2_send, a2_recv,
):
    reach = seq // 4
    chips = seq // 2
    units = reach + 1
    wide = reach // 2
    tall = chips // wide
    cols = hid.shape[1]
    heads = cols // HEAD
    span = cols // 128
    groups = units // GROUP
    scale = 1.0 / math.sqrt(HEAD)
    fold = scale * LOG2E

    own = lax.axis_index("seq")
    m = lax.axis_index("mp")
    chip = own // 2
    core = own % 2
    sib = own + 1 - 2 * core
    place = own % span
    base = own - place
    mine = slice(0, BLK)
    other = slice(BLK, 2 * BLK)
    x = chip % wide
    y = chip // wide
    earlier = jnp.minimum(reach, chip)

    def at_chip(to_x, to_y):
        return ((to_y * wide + to_x) * 2 + core, m)

    def load(src, dst, n):
        return pltpu.make_async_copy(src, dst, load_sem.at[n])

    loads = [
        load(k_h, kv.at[0, 0, mine], 0),
        load(v_h, kv.at[0, 1, mine], 1),
        load(hid_h, hid, 2),
        load(down_h, down, 3),
        load(up_h, up, 4),
        load(rq_h, rq, 5),
        load(do_h, do, 6),
        load(db_h, db, 7),
        load(da_h, da, 8),
    ]
    loads[0].start()
    loads[1].start()
    barrier = pltpu.get_barrier_semaphore()
    partners = [(own, (m + step) % mp) for step in range(1, mp)]
    partners += [(base + (place + step) % span, m) for step in range(1, span)]
    partners += [((own + span * step) % seq, m) for step in range(1, seq // span)]
    for peer in partners:
        pl.semaphore_signal(barrier, inc=1, device_id=peer, device_id_type=MESH)
    skips = wide - 1
    greeted = len(partners)
    if skips:
        greeted += jnp.where(x == skips, jnp.minimum(2, tall - 1 - y), 0)
        for dy in range(1, 3):

            @pl.when(jnp.logical_and(x == 0, y >= dy))
            def _():
                pl.semaphore_signal(
                    barrier, inc=1, device_id=at_chip(skips, y - dy), device_id_type=MESH
                )

    for n in (7, 8, 2, 3, 6, 4, 5):
        loads[n].start()
    loads[0].wait()
    loads[1].wait()
    pl.semaphore_wait(barrier, greeted)

    def exchange(buf, send, recv):
        copies = []
        for step in sorted(range(1, mp), key=lambda step: abs(step - mp // 2)):
            peer = (m + step) % mp
            copies.append(
                pltpu.make_async_remote_copy(
                    src_ref=buf.at[m], dst_ref=buf.at[m],
                    send_sem=send.at[step], recv_sem=recv.at[step],
                    device_id=(own, peer), device_id_type=MESH,
                )
            )
        return copies

    def column_copy(dy):
        return pltpu.make_async_remote_copy(
            src_ref=kv.at[0, :, mine], dst_ref=kv.at[dy * wide, :, mine],
            send_sem=col_send.at[dy], recv_sem=kv_recv.at[dy * wide],
            device_id=at_chip(x, y + dy), device_id_type=MESH,
        )

    def direct_copy(dy):
        e = dy * wide - skips
        return pltpu.make_async_remote_copy(
            src_ref=kv.at[0, :, mine], dst_ref=kv.at[e, :, mine],
            send_sem=direct_send.at[dy], recv_sem=kv_recv.at[e],
            device_id=at_chip(0, y + dy), device_id_type=MESH,
        )

    def direct(dy, act):
        if skips:

            @pl.when(jnp.logical_and(x == skips, y + dy < tall))
            def _():
                act(direct_copy(dy))

    def row_copy(dy, to_x):
        return pltpu.make_async_remote_copy(
            src_ref=kv.at[dy * wide, :, mine], dst_ref=kv.at[dy * wide + to_x - x, :, mine],
            send_sem=row_send.at[dy, to_x], recv_sem=kv_recv.at[dy * wide + to_x - x],
            device_id=at_chip(to_x, y), device_id_type=MESH,
        )

    def row_readers(dy, act):
        for to_x in range(wide):
            reads = (to_x > x, to_x != x, to_x < x)[dy]
            if dy and to_x == 0:
                reads = jnp.logical_and(reads, x != skips)

            @pl.when(jnp.logical_and(y >= dy, reads))
            def _():
                act(row_copy(dy, to_x))

    def kv_land(e):
        return pltpu.make_async_remote_copy(
            src_ref=kv.at[0, :, mine], dst_ref=kv.at[e, :, mine],
            send_sem=col_send.at[0], recv_sem=kv_recv.at[e],
            device_id=(sib, m), device_id_type=MESH,
        )

    def forward(e):
        return pltpu.make_async_remote_copy(
            src_ref=kv.at[e, :, mine], dst_ref=kv.at[e, :, other],
            send_sem=fwd_send.at[e], recv_sem=fwd_recv.at[e],
            device_id=(sib, m), device_id_type=MESH,
        )

    def forward_land(e):
        return pltpu.make_async_remote_copy(
            src_ref=kv.at[e, :, other], dst_ref=kv.at[e, :, other],
            send_sem=fwd_send.at[e], recv_sem=fwd_recv.at[e],
            device_id=(sib, m), device_id_type=MESH,
        )

    @pl.when(y + 1 < tall)
    def _():
        column_copy(1).start()

    forward(0).start()
    row_readers(0, lambda copy: copy.start())

    loads[7].wait()
    loads[8].wait()
    start = jnp.int32(0)
    first = jnp.int32(0)
    adapter = jnp.int32(0)
    bounds = []
    for d in range(docs):
        end = start + db[d]
        inside = jnp.logical_and(own >= start, own < end)
        first = jnp.where(inside, start, first)
        adapter = jnp.where(inside, da[d], adapter)
        bounds.append((start, end, da[d]))
        start = end

    loads[2].wait()
    loads[3].wait()
    lowx[m] = dot_nt(down[adapter], hid[...])
    low_copies = exchange(lowx, low_send, low_recv)
    for one in low_copies:
        one.start()

    @pl.when(y + 1 < tall)
    def _():
        column_copy(1).wait_send()

    @pl.when(y + 2 < tall)
    def _():
        column_copy(2).start()

    for dy in range(1, 3):
        direct(dy, lambda copy: copy.start())
    loads[6].wait()
    for h in range(heads):
        here = slice(h * BLK, (h + 1) * BLK)
        part = do[:, h * HEAD : (h + 1) * HEAD]
        dos[here, :] = part
        dot_t[:, here] = part.T

    size = select.shape
    row = lax.broadcasted_iota(jnp.int32, size, 0)
    col = lax.broadcasted_iota(jnp.int32, size, 1)
    same = (row % RANK) == (col % RANK)
    row_a = row // RANK
    col_s = base + col // RANK
    hit = jnp.zeros(size, F32)
    for begin, end, name in bounds:
        inside = jnp.logical_and(col_s >= begin, col_s < end)
        inside = jnp.logical_and(inside, row_a == name)
        hit = jnp.where(jnp.logical_and(inside, same), 1.0, hit)
    select[...] = hit.astype(BF16)

    @pl.loop(earlier + 1, units)
    def _(e):
        kv[e] = jnp.zeros(kv.shape[1:], BF16)

    for dy in range(1, 3):

        @pl.when(y >= dy)
        def _():
            kv_land(dy * wide).wait_recv()
            forward(dy * wide).start()

        row_readers(dy, lambda copy: copy.start())

    @pl.loop(1, x + 1)
    def _(e):
        kv_land(e).wait_recv()
        forward(e).start()

    loads[4].wait()
    loads[5].wait()
    up_rows = up[adapter]
    for one in low_copies:
        one.wait_recv()
    low_sum = lowx[0]
    for step in range(1, mp):
        low_sum = low_sum + lowx[step]
    low_t = low_sum.astype(BF16)
    low = low_sum.T.astype(BF16)
    for h in range(heads):
        part = slice(h * HEAD, (h + 1) * HEAD)
        here = slice(h * BLK, (h + 1) * BLK)
        q = (rq[:, part].astype(F32) + dot(low, up_rows[:, part])).astype(BF16)
        qs[here, :] = q
        qt[:, here] = q.T

    below = lax.broadcasted_iota(jnp.int32, (BLK, cols), 0) <= (
        lax.broadcasted_iota(jnp.int32, (BLK, cols), 1) % BLK
    )
    turn_of = {}

    def score(turn, halves):
        keys = jnp.concatenate([kv[e, 0, h * BLK : (h + 1) * BLK] for e, h in halves], axis=0)
        values = jnp.concatenate([kv[e, 1, h * BLK : (h + 1) * BLK] for e, h in halves], axis=0)
        s_all = dot(keys, qt[...])
        dp_all = dot(values, dot_t[...])
        keys_all = keys.T
        values_all = values.T
        parts = []
        top = None if turn == 0 else stat[0:1, :]
        for n, (e, h) in enumerate(halves):
            turn_of[e, h] = turn
            here = slice(n * BLK, (n + 1) * BLK)
            half = slice(h * BLK, (h + 1) * BLK)
            keys_t[e, :, half] = keys_all[:, here]
            vals_t[e, :, half] = values_all[:, here]
            block = 2 * (chip - e) + (core if h == 0 else 1 - core)
            seen = jnp.logical_and(block >= first, block <= own)
            s = s_all[here]
            if e == 0 and h == 0:
                s = jnp.where(below, s, NEG)
            off = jnp.where(seen, 0.0, -NEG)
            high = jnp.max(s, axis=0, keepdims=True) - off
            top = high if top is None else jnp.maximum(top, high)
            parts.append((e, half, s, dp_all[here], off))
        shift = top * fold
        total = delta = None
        if turn:
            shrink = jnp.exp2(stat[0:1, :] * fold - shift)
            total = shrink * stat[8:9, :]
            delta = shrink * stat[16:17, :]
        for e, half, s, dp, off in parts:
            p = jnp.exp2(s * fold - (shift + off))
            sbuf[e, half, :] = p
            dpbuf[e, half, :] = dp
            row_sum = jnp.sum(p, axis=0, keepdims=True)
            row_delta = jnp.sum(p * dp, axis=0, keepdims=True)
            total = row_sum if total is None else total + row_sum
            delta = row_delta if delta is None else delta + row_delta
        stat[0:1, :] = top
        stat[8:9, :] = total
        stat[16:17, :] = delta
        shifts[turn : turn + 1, :] = shift

    forward_land(0).wait_recv()
    for dy in range(1, 3):

        @pl.when(y >= dy)
        def _():
            forward_land(dy * wide).wait_recv()

    score(0, [(dy * wide, h) for dy in range(3) for h in range(2)])
    turns = 1
    for dy in range(2):
        near = [dy * wide + step for step in range(1, wide)]
        for e in near:

            @pl.when(jnp.logical_and(e > x, e <= earlier))
            def _():
                kv_land(e).wait_recv()
                forward(e).start()

        if near:
            score(turns, [(e, 0) for e in near])
        for e in near:

            @pl.when(e <= earlier)
            def _():
                forward_land(e).wait_recv()

        if near:
            score(turns + 1, [(e, 1) for e in near])
        turns += 2

    total = stat[8:9, :]
    shifts[8:16, :] = jnp.exp2(
        shifts[0:8, :] - (stat[0:1, :] * fold + jnp.log(total) * LOG2E)
    )
    stat[16:17, :] = stat[16:17, :] / total
    for e in range(units):
        for h in range(2):
            half = slice(h * BLK, (h + 1) * BLK)
            here = slice((2 * e + h) * BLK, (2 * e + h + 1) * BLK)
            factor = 8 + turn_of[e, h]
            for at in range(0, cols, NARROW):
                part = slice(at, at + NARROW)
                p = sbuf[e, half, part] * shifts[factor : factor + 1, part]
                ds = p * (dpbuf[e, half, part] - stat[16:17, part])
                dsbuf[here, part] = ds.astype(BF16)
                pbuf[here, part] = p.astype(BF16)

    def all_units(turned):
        return jnp.concatenate([turned[e] for e in range(units)], axis=1)

    dq_t = dot(all_units(keys_t), dsbuf[...]) * scale
    for h in range(heads):
        part = slice(h * HEAD, (h + 1) * HEAD)
        gqv[:, part] = dq_t[:, h * BLK : (h + 1) * BLK].T.astype(BF16)
    dlowx[m] = dot_nt(up_rows, gqv[...])
    dlow_copies = exchange(dlowx, dlow_send, dlow_recv)
    for one in dlow_copies:
        one.start()

    own16 = pl.ds(pl.multiple_of(own * RANK, RANK), RANK)
    place16 = pl.ds(pl.multiple_of(place * RANK, RANK), RANK)
    rest1 = pl.ds(0, (span - 1) * RANK)
    rest2 = pl.ds(0, (seq - 1) * RANK)

    def spread(kind, product):
        for t in range(span):
            piece[kind, t] = product[:, t * 128 : (t + 1) * 128].astype(BF16)

        @pl.loop(1, span)
        def _(step):
            peer = (place + step) % span
            pltpu.make_async_remote_copy(
                src_ref=piece.at[kind, peer], dst_ref=got.at[kind, place16],
                send_sem=a1_send.at[kind], recv_sem=a1_recv.at[kind],
                device_id=(base + peer, m), device_id_type=MESH,
            ).start()

    def settle(kind):
        land = got.at[kind, rest1]
        pltpu.make_async_copy(land, land, a1_recv.at[kind]).wait()
        got[kind, place16, :] = piece[kind, place]
        red[kind] = dot(select[...], got[kind]).astype(BF16)

        @pl.loop(0, seq - 1)
        def _(step):
            peer = (own + 1 + (step + seq // 2 - 1) % (seq - 1)) % seq
            pltpu.make_async_remote_copy(
                src_ref=red.at[kind, pl.ds(pl.multiple_of(peer * RANK, RANK), RANK)],
                dst_ref=fin.at[kind, own16],
                send_sem=a2_send.at[kind], recv_sem=a2_recv.at[kind],
                device_id=(peer, m), device_id_type=MESH,
            ).start()

    def finish(kind):
        land = fin.at[kind, rest2]
        pltpu.make_async_copy(land, land, a2_recv.at[kind]).wait()
        fin[kind, own16, :] = red[kind, own16, :]
        for t in range(span):
            whole = jnp.zeros((RANK, 128), F32)
            for line in range(seq // span):
                at = (line * span + t) * RANK
                whole = whole + fin[kind, at : at + RANK, :].astype(F32)
            (gb, ga)[kind][0, :, t * 128 : (t + 1) * 128] = whole

    def sib_copy(g):
        return pltpu.make_async_remote_copy(
            src_ref=sib_out.at[g], dst_ref=sib_in.at[g],
            send_sem=sib_send.at[g], recv_sem=sib_recv.at[g],
            device_id=(sib, m), device_id_type=MESH,
        )

    def merge_copy(e):
        owner = chip - e
        to_x = owner % wide
        dy = y - owner // wide
        return to_x, pltpu.make_async_remote_copy(
            src_ref=dkv_out.at[e], dst_ref=dkv_in.at[dy, x],
            send_sem=dkv_send.at[e], recv_sem=dkv_recv.at[dy, x],
            device_id=at_chip(to_x, y), device_id_type=MESH,
        )

    def merge_land(dy, from_x):
        return pltpu.make_async_remote_copy(
            src_ref=dkv_out.at[0], dst_ref=dkv_in.at[dy, from_x],
            send_sem=dkv_send.at[0], recv_sem=dkv_recv.at[dy, from_x],
            device_id=(sib, m), device_id_type=MESH,
        )

    def home_copy(dy):
        return pltpu.make_async_remote_copy(
            src_ref=home_out.at[dy], dst_ref=home_in.at[dy],
            send_sem=home_send.at[dy], recv_sem=home_recv.at[dy],
            device_id=at_chip(x, y - dy), device_id_type=MESH,
        )

    def merge_row(dy):
        for from_x in range(wide):
            writes = (from_x > x, from_x != x, from_x < x)[dy]

            @pl.when(jnp.logical_and(y >= dy, writes))
            def _():
                merge_land(dy, from_x).wait_recv()
                total_kv[dy] = total_kv[dy] + dkv_in[dy, from_x].astype(F32)

    def weigh(g):
        here = slice(g * GROUP * 2 * BLK, (g + 1) * GROUP * 2 * BLK)
        pair[0] = dot(dsbuf[here, :], qs[...]) * scale
        pair[1] = dot(pbuf[here, :], dos[...])
        for k in range(GROUP):
            for kind in range(2):
                at = 2 * k * BLK
                own_st[g, k, kind] = pair[kind, at : at + BLK, :]
                sib_out[g, k, kind] = pair[kind, at + BLK : at + 2 * BLK, :].astype(BF16)
        sib_copy(g).start()

    def pass_on(g):
        sib_copy(g).wait_recv()
        for k in range(GROUP - 1, -1, -1):
            e = g * GROUP + k
            merged = own_st[g, k] + sib_in[g, k].astype(F32)
            if e % wide == 0:
                total_kv[e // wide] = merged
            else:
                dkv_out[e] = merged.astype(BF16)
                to_x, copy = merge_copy(e)

                @pl.when(e <= earlier)
                def _():
                    copy.start()

    spread(0, dot(low_t, gqv[...]))
    for g in range(groups - 1, -1, -1):
        weigh(g)
        if g < groups - 1:
            pass_on(g + 1)

    for one in dlow_copies:
        one.wait_recv()
    dlow_sum = dlowx[0]
    for step in range(1, mp):
        dlow_sum = dlow_sum + dlowx[step]
    spread(1, dot(dlow_sum.astype(BF16), hid[...]))
    pass_on(0)
    settle(0)

    out_t = dot(all_units(vals_t), pbuf[...])
    for h in range(heads):
        part = slice(h * HEAD, (h + 1) * HEAD)
        outv[:, part] = out_t[:, part].T.astype(BF16)

    def send_home(dy):
        merge_row(dy)

        @pl.when(y >= dy)
        def _():
            home_out[dy] = total_kv[dy].astype(BF16)
            home_copy(dy).start()

    send_home(2)
    settle(1)
    send_home(1)
    merge_row(0)
    finish(0)
    for dy in range(1, 3):

        @pl.when(y + dy < tall)
        def _():
            home_copy(dy).wait_recv()
            total_kv[0] = total_kv[0] + home_in[dy].astype(F32)

    gk[...] = total_kv[0, 0].astype(BF16)
    gv[...] = total_kv[0, 1].astype(BF16)

    finish(1)

    for one in low_copies + dlow_copies:
        one.wait_send()

    for dy in range(3):
        row_readers(dy, lambda copy: copy.wait_send())
    for dy in range(1, 3):

        @pl.when(y >= dy)
        def _():
            home_copy(dy).wait_send()

    @pl.when(y + 2 < tall)
    def _():
        column_copy(2).wait_send()

    for dy in range(1, 3):
        direct(dy, lambda copy: copy.wait_send())

    @pl.loop(0, earlier + 1)
    def _(e):
        forward(e).wait_send()

    for g in range(groups):
        sib_copy(g).wait_send()
    for e in range(units):
        if e % wide:
            to_x, copy = merge_copy(e)

            @pl.when(e <= earlier)
            def _():
                copy.wait_send()

    for kind in range(2):
        sent = got.at[kind, rest1]
        pltpu.make_async_copy(sent, sent, a1_send.at[kind]).wait()
        sent = red.at[kind, rest2]
        pltpu.make_async_copy(sent, sent, a2_send.at[kind]).wait()


def place_kernel(count, *refs):
    sems = refs[2 * count]
    copies = [
        pltpu.make_async_copy(refs[n], refs[count + n], sems.at[n]) for n in range(count)
    ]
    for one in copies:
        one.start()
    for one in copies:
        one.wait()


def on_device(
    hidden_rows, rotated_queries, rotated_keys, value_rows, adapter_down, adapter_up,
    output_gradient, document_blocks, document_adapter,
):
    seq = lax.axis_size("seq")
    mp = lax.axis_size("mp")
    rows, cols = hidden_rows.shape
    adapters = adapter_down.shape[0]
    units = seq // 4 + 1
    wide = seq // 8
    span = cols // 128
    groups = units // GROUP
    docs = document_blocks.shape[0]
    any_space = pl.BlockSpec(memory_space=pl.ANY)
    dma = pltpu.SemaphoreType.DMA
    vmem = pltpu.VMEM
    shapes = (
        jax.ShapeDtypeStruct((rows, cols), BF16),
        jax.ShapeDtypeStruct((rows, cols), BF16),
        jax.ShapeDtypeStruct((rows, HEAD), BF16),
        jax.ShapeDtypeStruct((rows, HEAD), BF16),
        jax.ShapeDtypeStruct((1, RANK, cols), F32),
        jax.ShapeDtypeStruct((1, RANK, cols), F32),
    )
    made = pl.pallas_call(
        functools.partial(kernel, seq, mp, docs),
        out_shape=[vmem(one.shape, one.dtype) for one in shapes],
        in_specs=[any_space] * 9,
        out_specs=[pl.BlockSpec(memory_space=pltpu.VMEM)] * 6,
        scratch_shapes=[
            pltpu.SMEM((docs,), jnp.int32),
            pltpu.SMEM((docs,), jnp.int32),
            vmem((rows, cols), BF16),
            vmem((rows, cols), BF16),
            vmem((adapters, RANK, cols), BF16),
            vmem((adapters, RANK, cols), BF16),
            vmem((rows, cols), BF16),
            vmem((units, 2, 2 * BLK, HEAD), BF16),
            vmem((cols, HEAD), BF16),
            vmem((HEAD, cols), BF16),
            vmem((cols, HEAD), BF16),
            vmem((HEAD, cols), BF16),
            vmem((units, 2 * BLK, cols), F32),
            vmem((units, 2 * BLK, cols), F32),
            vmem((units * 2 * BLK, cols), BF16),
            vmem((units * 2 * BLK, cols), BF16),
            vmem((mp, RANK, rows), F32),
            vmem((mp, RANK, rows), F32),
            vmem((24, cols), F32),
            vmem((16, cols), F32),
            vmem((units, HEAD, 2 * BLK), BF16),
            vmem((units, HEAD, 2 * BLK), BF16),
            vmem((2, GROUP * 2 * BLK, HEAD), F32),
            vmem((groups, GROUP, 2, BLK, HEAD), F32),
            vmem((groups, GROUP, 2, BLK, HEAD), BF16),
            vmem((groups, GROUP, 2, BLK, HEAD), BF16),
            vmem((units, 2, BLK, HEAD), BF16),
            vmem((3, wide, 2, BLK, HEAD), BF16),
            vmem((3, 2, BLK, HEAD), BF16),
            vmem((3, 2, BLK, HEAD), BF16),
            vmem((3, 2, BLK, HEAD), F32),
            vmem((adapters * RANK, span * RANK), BF16),
            vmem((2, span, RANK, 128), BF16),
            vmem((2, span * RANK, 128), BF16),
            vmem((2, seq * RANK, 128), BF16),
            vmem((2, seq * RANK, 128), BF16),
            dma((9,)),
            dma((mp,)), dma((mp,)), dma((mp,)), dma((mp,)),
            dma((3,)), dma((3, wide)), dma((3,)), dma((units,)), dma((units,)), dma((units,)),
            dma((groups,)), dma((groups,)), dma((units,)), dma((3, wide)),
            dma((3,)), dma((3,)),
            dma((2,)), dma((2,)), dma((2,)), dma((2,)),
        ],
        compiler_params=pltpu.CompilerParams(
            collective_id=0, has_side_effects=True, vmem_limit_bytes=48 * 1024 * 1024
        ),
    )(
        *(
            pltpu.with_memory_space_constraint(one, pltpu.HBM)
            for one in (
                document_blocks, document_adapter, hidden_rows, rotated_queries, rotated_keys,
                value_rows, adapter_down, adapter_up, output_gradient,
            )
        )
    )
    return pl.pallas_call(
        functools.partial(place_kernel, len(shapes)),
        out_shape=shapes,
        in_specs=[any_space] * len(shapes),
        out_specs=[any_space] * len(shapes),
        scratch_shapes=[dma((len(shapes),))],
    )(*(pltpu.with_memory_space_constraint(one, pltpu.VMEM) for one in made))


def solution(mesh):
    return jax.shard_map(
        on_device,
        mesh=mesh,
        in_specs=(
            P("seq", "mp"),
            P("seq", "mp"),
            P("seq", "mp"),
            P("seq", "mp"),
            P(None, None, "mp"),
            P(None, None, "mp"),
            P("seq", "mp"),
            P(),
            P(),
        ),
        out_specs=(
            P("seq", "mp"),
            P("seq", "mp"),
            P("seq", "mp"),
            P("seq", "mp"),
            P("seq", None, "mp"),
            P("seq", None, "mp"),
        ),
        check_vma=False,
    )
```

```python
import functools
import math

import jax
import jax.numpy as jnp
from jax import lax
from jax.experimental import pallas as pl
from jax.experimental.pallas import tpu as pltpu
from jax.sharding import PartitionSpec as P

HEAD = 128
BLK = 128
RANK = 16
NARROW = 256
GROUP = 3
NEG = -1e30
LOG2E = 1.4426950408889634
MESH = pl.DeviceIdType.MESH
F32 = jnp.float32
BF16 = jnp.bfloat16

NT = (((1,), (1,)), ((), ()))


def dot(a, b):
    return jnp.dot(a, b, preferred_element_type=F32)


def dot_nt(a, b):
    return lax.dot_general(a, b, NT, preferred_element_type=F32)


def kernel(
    seq, mp, docs,
    db_h, da_h, hid_h, rq_h, k_h, v_h, down_h, up_h, do_h,
    outv, gqv, gk, gv, ga, gb,
    db, da, hid, rq, down, up, do, kv, qs, qt, dos, dot_t, sbuf, dpbuf, pbuf, dsbuf,
    lowx, dlowx, stat, shifts, keys_t, vals_t, pair, own_st, sib_out, sib_in,
    dkv_out, dkv_in, home_out, home_in, total_kv, select, piece, got, red, fin,
    load_sem,
    low_send, low_recv, dlow_send, dlow_recv,
    col_send, row_send, direct_send, kv_recv, fwd_send, fwd_recv, sib_send, sib_recv, dkv_send, dkv_recv,
    home_send, home_recv,
    a1_send, a1_recv, a2_send, a2_recv,
):
    reach = seq // 4
    chips = seq // 2
    units = reach + 1
    wide = reach // 2
    tall = chips // wide
    cols = hid.shape[1]
    heads = cols // HEAD
    span = cols // 128
    groups = units // GROUP
    scale = 1.0 / math.sqrt(HEAD)
    fold = scale * LOG2E

    own = lax.axis_index("seq")
    m = lax.axis_index("mp")
    chip = own // 2
    core = own % 2
    sib = own + 1 - 2 * core
    mine = slice(0, BLK)
    other = slice(BLK, 2 * BLK)
    x = chip % wide
    y = chip // wide
    tier = span // 2
    place = (y % tier) * 2 + core
    level = y - y % tier

    def member(p):
        return ((level + p // 2) * wide + x) * 2 + p % 2
    earlier = jnp.minimum(reach, chip)

    def at_chip(to_x, to_y):
        return ((to_y * wide + to_x) * 2 + core, m)

    def load(src, dst, n):
        return pltpu.make_async_copy(src, dst, load_sem.at[n])

    loads = [
        load(k_h, kv.at[0, 0, mine], 0),
        load(v_h, kv.at[0, 1, mine], 1),
        load(hid_h, hid, 2),
        load(down_h, down, 3),
        load(up_h, up, 4),
        load(rq_h, rq, 5),
        load(do_h, do, 6),
        load(db_h, db, 7),
        load(da_h, da, 8),
    ]
    loads[0].start()
    loads[1].start()
    barrier = pltpu.get_barrier_semaphore()
    partners = [(own, (m + step) % mp) for step in range(1, mp)]
    partners += [(sib, m)]
    partners += [at_chip(x, (y + step) % tall) for step in range(1, tall)]
    partners += [(member((place + 2 * step + 1 - 2 * core) % span), m) for step in range(1, tier)]
    partners += [at_chip((x + step) % wide, y) for step in range(1, wide)]
    for peer in partners:
        pl.semaphore_signal(barrier, inc=1, device_id=peer, device_id_type=MESH)
    skips = wide - 1
    greeted = len(partners)
    if skips:
        greeted += jnp.where(x == skips, jnp.minimum(2, tall - 1 - y), 0)
        for dy in range(1, 3):

            @pl.when(jnp.logical_and(x == 0, y >= dy))
            def _():
                pl.semaphore_signal(
                    barrier, inc=1, device_id=at_chip(skips, y - dy), device_id_type=MESH
                )

    for n in (7, 8, 2, 3, 6, 4, 5):
        loads[n].start()
    loads[0].wait()
    loads[1].wait()
    pl.semaphore_wait(barrier, greeted)

    def exchange(buf, send, recv):
        copies = []
        for step in sorted(range(1, mp), key=lambda step: abs(step - mp // 2)):
            peer = (m + step) % mp
            copies.append(
                pltpu.make_async_remote_copy(
                    src_ref=buf.at[m], dst_ref=buf.at[m],
                    send_sem=send.at[step], recv_sem=recv.at[step],
                    device_id=(own, peer), device_id_type=MESH,
                )
            )
        return copies

    def column_copy(dy):
        return pltpu.make_async_remote_copy(
            src_ref=kv.at[0, :, mine], dst_ref=kv.at[dy * wide, :, mine],
            send_sem=col_send.at[dy], recv_sem=kv_recv.at[dy * wide],
            device_id=at_chip(x, y + dy), device_id_type=MESH,
        )

    def direct_copy(dy):
        e = dy * wide - skips
        return pltpu.make_async_remote_copy(
            src_ref=kv.at[0, :, mine], dst_ref=kv.at[e, :, mine],
            send_sem=direct_send.at[dy], recv_sem=kv_recv.at[e],
            device_id=at_chip(0, y + dy), device_id_type=MESH,
        )

    def direct(dy, act):
        if skips:

            @pl.when(jnp.logical_and(x == skips, y + dy < tall))
            def _():
                act(direct_copy(dy))

    def row_copy(dy, to_x):
        return pltpu.make_async_remote_copy(
            src_ref=kv.at[dy * wide, :, mine], dst_ref=kv.at[dy * wide + to_x - x, :, mine],
            send_sem=row_send.at[dy, to_x], recv_sem=kv_recv.at[dy * wide + to_x - x],
            device_id=at_chip(to_x, y), device_id_type=MESH,
        )

    def row_readers(dy, act):
        for to_x in range(wide):
            reads = (to_x > x, to_x != x, to_x < x)[dy]
            if dy and to_x == 0:
                reads = jnp.logical_and(reads, x != skips)

            @pl.when(jnp.logical_and(y >= dy, reads))
            def _():
                act(row_copy(dy, to_x))

    def kv_land(e):
        return pltpu.make_async_remote_copy(
            src_ref=kv.at[0, :, mine], dst_ref=kv.at[e, :, mine],
            send_sem=col_send.at[0], recv_sem=kv_recv.at[e],
            device_id=(sib, m), device_id_type=MESH,
        )

    def forward(e):
        return pltpu.make_async_remote_copy(
            src_ref=kv.at[e, :, mine], dst_ref=kv.at[e, :, other],
            send_sem=fwd_send.at[e], recv_sem=fwd_recv.at[e],
            device_id=(sib, m), device_id_type=MESH,
        )

    def forward_land(e):
        return pltpu.make_async_remote_copy(
            src_ref=kv.at[e, :, other], dst_ref=kv.at[e, :, other],
            send_sem=fwd_send.at[e], recv_sem=fwd_recv.at[e],
            device_id=(sib, m), device_id_type=MESH,
        )

    @pl.when(y + 1 < tall)
    def _():
        column_copy(1).start()

    forward(0).start()
    row_readers(0, lambda copy: copy.start())

    loads[7].wait()
    loads[8].wait()
    start = jnp.int32(0)
    first = jnp.int32(0)
    adapter = jnp.int32(0)
    bounds = []
    for d in range(docs):
        end = start + db[d]
        inside = jnp.logical_and(own >= start, own < end)
        first = jnp.where(inside, start, first)
        adapter = jnp.where(inside, da[d], adapter)
        bounds.append((start, end, da[d]))
        start = end

    loads[2].wait()
    loads[3].wait()
    lowx[m] = dot_nt(down[adapter], hid[...])
    low_copies = exchange(lowx, low_send, low_recv)
    for one in low_copies:
        one.start()

    @pl.when(y + 1 < tall)
    def _():
        column_copy(1).wait_send()

    @pl.when(y + 2 < tall)
    def _():
        column_copy(2).start()

    for dy in range(1, 3):
        direct(dy, lambda copy: copy.start())
    loads[6].wait()
    for h in range(heads):
        here = slice(h * BLK, (h + 1) * BLK)
        part = do[:, h * HEAD : (h + 1) * HEAD]
        dos[here, :] = part
        dot_t[:, here] = part.T

    size = select.shape
    row = lax.broadcasted_iota(jnp.int32, size, 0)
    col = lax.broadcasted_iota(jnp.int32, size, 1)
    same = (row % RANK) == (col % RANK)
    row_a = row // RANK
    col_s = member(col // RANK)
    hit = jnp.zeros(size, F32)
    for begin, end, name in bounds:
        inside = jnp.logical_and(col_s >= begin, col_s < end)
        inside = jnp.logical_and(inside, row_a == name)
        hit = jnp.where(jnp.logical_and(inside, same), 1.0, hit)
    select[...] = hit.astype(BF16)

    @pl.loop(earlier + 1, units)
    def _(e):
        kv[e] = jnp.zeros(kv.shape[1:], BF16)

    for dy in range(1, 3):

        @pl.when(y >= dy)
        def _():
            kv_land(dy * wide).wait_recv()
            forward(dy * wide).start()

        row_readers(dy, lambda copy: copy.start())

    @pl.loop(1, x + 1)
    def _(e):
        kv_land(e).wait_recv()
        forward(e).start()

    loads[4].wait()
    loads[5].wait()
    up_rows = up[adapter]
    for one in low_copies:
        one.wait_recv()
    low_sum = lowx[0]
    for step in range(1, mp):
        low_sum = low_sum + lowx[step]
    low_t = low_sum.astype(BF16)
    low = low_sum.T.astype(BF16)
    for h in range(heads):
        part = slice(h * HEAD, (h + 1) * HEAD)
        here = slice(h * BLK, (h + 1) * BLK)
        q = (rq[:, part].astype(F32) + dot(low, up_rows[:, part])).astype(BF16)
        qs[here, :] = q
        qt[:, here] = q.T

    below = lax.broadcasted_iota(jnp.int32, (BLK, cols), 0) <= (
        lax.broadcasted_iota(jnp.int32, (BLK, cols), 1) % BLK
    )
    turn_of = {}

    def score(turn, halves):
        keys = jnp.concatenate([kv[e, 0, h * BLK : (h + 1) * BLK] for e, h in halves], axis=0)
        values = jnp.concatenate([kv[e, 1, h * BLK : (h + 1) * BLK] for e, h in halves], axis=0)
        s_all = dot(keys, qt[...])
        dp_all = dot(values, dot_t[...])
        keys_all = keys.T
        values_all = values.T
        parts = []
        top = None if turn == 0 else stat[0:1, :]
        for n, (e, h) in enumerate(halves):
            turn_of[e, h] = turn
            here = slice(n * BLK, (n + 1) * BLK)
            half = slice(h * BLK, (h + 1) * BLK)
            keys_t[e, :, half] = keys_all[:, here]
            vals_t[e, :, half] = values_all[:, here]
            block = 2 * (chip - e) + (core if h == 0 else 1 - core)
            seen = jnp.logical_and(block >= first, block <= own)
            s = s_all[here]
            if e == 0 and h == 0:
                s = jnp.where(below, s, NEG)
            off = jnp.where(seen, 0.0, -NEG)
            high = jnp.max(s, axis=0, keepdims=True) - off
            top = high if top is None else jnp.maximum(top, high)
            parts.append((e, half, s, dp_all[here], off))
        shift = top * fold
        total = delta = None
        if turn:
            shrink = jnp.exp2(stat[0:1, :] * fold - shift)
            total = shrink * stat[8:9, :]
            delta = shrink * stat[16:17, :]
        for e, half, s, dp, off in parts:
            p = jnp.exp2(s * fold - (shift + off))
            sbuf[e, half, :] = p
            dpbuf[e, half, :] = dp
            row_sum = jnp.sum(p, axis=0, keepdims=True)
            row_delta = jnp.sum(p * dp, axis=0, keepdims=True)
            total = row_sum if total is None else total + row_sum
            delta = row_delta if delta is None else delta + row_delta
        stat[0:1, :] = top
        stat[8:9, :] = total
        stat[16:17, :] = delta
        shifts[turn : turn + 1, :] = shift

    forward_land(0).wait_recv()
    for dy in range(1, 3):

        @pl.when(y >= dy)
        def _():
            forward_land(dy * wide).wait_recv()

    score(0, [(dy * wide, h) for dy in range(3) for h in range(2)])
    turns = 1
    for dy in range(2):
        near = [dy * wide + step for step in range(1, wide)]
        for e in near:

            @pl.when(jnp.logical_and(e > x, e <= earlier))
            def _():
                kv_land(e).wait_recv()
                forward(e).start()

        if near:
            score(turns, [(e, 0) for e in near])
        for e in near:

            @pl.when(e <= earlier)
            def _():
                forward_land(e).wait_recv()

        if near:
            score(turns + 1, [(e, 1) for e in near])
        turns += 2

    total = stat[8:9, :]
    shifts[8:16, :] = jnp.exp2(
        shifts[0:8, :] - (stat[0:1, :] * fold + jnp.log(total) * LOG2E)
    )
    stat[16:17, :] = stat[16:17, :] / total
    for e in range(units):
        for h in range(2):
            half = slice(h * BLK, (h + 1) * BLK)
            here = slice((2 * e + h) * BLK, (2 * e + h + 1) * BLK)
            factor = 8 + turn_of[e, h]
            for at in range(0, cols, NARROW):
                part = slice(at, at + NARROW)
                p = sbuf[e, half, part] * shifts[factor : factor + 1, part]
                ds = p * (dpbuf[e, half, part] - stat[16:17, part])
                dsbuf[here, part] = ds.astype(BF16)

    def all_units(turned):
        return jnp.concatenate([turned[e] for e in range(units)], axis=1)

    dq_t = dot(all_units(keys_t), dsbuf[...]) * scale
    for h in range(heads):
        part = slice(h * HEAD, (h + 1) * HEAD)
        gqv[:, part] = dq_t[:, h * BLK : (h + 1) * BLK].T.astype(BF16)
    dlowx[m] = dot_nt(up_rows, gqv[...])
    dlow_copies = exchange(dlowx, dlow_send, dlow_recv)
    for one in dlow_copies:
        one.start()

    own16 = pl.ds(pl.multiple_of(own * RANK, RANK), RANK)
    place16 = pl.ds(pl.multiple_of(place * RANK, RANK), RANK)
    rest1 = pl.ds(0, (span - 1) * RANK)
    rest2 = pl.ds(0, (seq - 1) * RANK)

    def spread(kind, product):
        for t in range(span):
            piece[kind, t] = product[:, t * 128 : (t + 1) * 128].astype(BF16)

        @pl.loop(1, span)
        def _(step):
            peer = (place + step) % span
            pltpu.make_async_remote_copy(
                src_ref=piece.at[kind, peer], dst_ref=got.at[kind, place16],
                send_sem=a1_send.at[kind], recv_sem=a1_recv.at[kind],
                device_id=(member(peer), m), device_id_type=MESH,
            ).start()

    def settle(kind):
        land = got.at[kind, rest1]
        pltpu.make_async_copy(land, land, a1_recv.at[kind]).wait()
        got[kind, place16, :] = piece[kind, place]
        red[kind] = dot(select[...], got[kind]).astype(BF16)

        for step in sorted(range(1, seq), key=lambda step: abs(step - seq // 2 - wide // 2)):
            peer = own + step
            peer = jnp.where(peer >= seq, peer - seq, peer)
            pltpu.make_async_remote_copy(
                src_ref=red.at[kind, pl.ds(pl.multiple_of(peer * RANK, RANK), RANK)],
                dst_ref=fin.at[kind, own16],
                send_sem=a2_send.at[kind], recv_sem=a2_recv.at[kind],
                device_id=(peer, m), device_id_type=MESH,
            ).start()

    def finish(kind):
        land = fin.at[kind, rest2]
        pltpu.make_async_copy(land, land, a2_recv.at[kind]).wait()
        fin[kind, own16, :] = red[kind, own16, :]
        for t in range(span):
            whole = jnp.zeros((RANK, 128), F32)
            for line in range(seq // span):
                line_y = line // wide * tier + t // 2
                at = ((line_y * wide + line % wide) * 2 + t % 2) * RANK
                whole = whole + fin[kind, at : at + RANK, :].astype(F32)
            (gb, ga)[kind][0, :, t * 128 : (t + 1) * 128] = whole

    def sib_copy(g):
        return pltpu.make_async_remote_copy(
            src_ref=sib_out.at[g], dst_ref=sib_in.at[g],
            send_sem=sib_send.at[g], recv_sem=sib_recv.at[g],
            device_id=(sib, m), device_id_type=MESH,
        )

    def merge_copy(e):
        owner = chip - e
        to_x = owner % wide
        dy = y - owner // wide
        return to_x, pltpu.make_async_remote_copy(
            src_ref=dkv_out.at[e], dst_ref=dkv_in.at[dy, x],
            send_sem=dkv_send.at[e], recv_sem=dkv_recv.at[dy, x],
            device_id=at_chip(to_x, y), device_id_type=MESH,
        )

    def merge_land(dy, from_x):
        return pltpu.make_async_remote_copy(
            src_ref=dkv_out.at[0], dst_ref=dkv_in.at[dy, from_x],
            send_sem=dkv_send.at[0], recv_sem=dkv_recv.at[dy, from_x],
            device_id=(sib, m), device_id_type=MESH,
        )

    def home_copy(dy):
        return pltpu.make_async_remote_copy(
            src_ref=home_out.at[dy], dst_ref=home_in.at[dy],
            send_sem=home_send.at[dy], recv_sem=home_recv.at[dy],
            device_id=at_chip(x, y - dy), device_id_type=MESH,
        )

    def merge_row(dy):
        for from_x in range(wide):
            writes = (from_x > x, from_x != x, from_x < x)[dy]

            @pl.when(jnp.logical_and(y >= dy, writes))
            def _():
                merge_land(dy, from_x).wait_recv()
                total_kv[dy] = total_kv[dy] + dkv_in[dy, from_x].astype(F32)

    def fix(g):
        for e in range(g * GROUP, (g + 1) * GROUP):
            for h in range(2):
                half = slice(h * BLK, (h + 1) * BLK)
                here = slice((2 * e + h) * BLK, (2 * e + h + 1) * BLK)
                factor = 8 + turn_of[e, h]
                for at in range(0, cols, NARROW):
                    part = slice(at, at + NARROW)
                    p = sbuf[e, half, part] * shifts[factor : factor + 1, part]
                    pbuf[here, part] = p.astype(BF16)

    def weigh(g):
        fix(g)
        here = slice(g * GROUP * 2 * BLK, (g + 1) * GROUP * 2 * BLK)
        pair[0] = dot(dsbuf[here, :], qs[...]) * scale
        pair[1] = dot(pbuf[here, :], dos[...])
        for k in range(GROUP):
            for kind in range(2):
                at = 2 * k * BLK
                own_st[g, k, kind] = pair[kind, at : at + BLK, :]
                sib_out[g, k, kind] = pair[kind, at + BLK : at + 2 * BLK, :].astype(BF16)
        sib_copy(g).start()

    def pass_on(g):
        sib_copy(g).wait_recv()
        for k in range(GROUP - 1, -1, -1):
            e = g * GROUP + k
            merged = own_st[g, k] + sib_in[g, k].astype(F32)
            if e % wide == 0:
                total_kv[e // wide] = merged
            else:
                dkv_out[e] = merged.astype(BF16)
                to_x, copy = merge_copy(e)

                @pl.when(e <= earlier)
                def _():
                    copy.start()

    for g in range(groups - 1, -1, -1):
        weigh(g)
        if g == groups - 2 or groups == 1:
            spread(0, dot(low_t, gqv[...]))
        if g < groups - 1:
            pass_on(g + 1)
    pass_on(0)

    for one in dlow_copies:
        one.wait_recv()
    dlow_sum = dlowx[0]
    for step in range(1, mp):
        dlow_sum = dlow_sum + dlowx[step]
    spread(1, dot(dlow_sum.astype(BF16), hid[...]))
    settle(0)

    out_t = dot(all_units(vals_t), pbuf[...])
    for h in range(heads):
        part = slice(h * HEAD, (h + 1) * HEAD)
        outv[:, part] = out_t[:, part].T.astype(BF16)

    def send_home(dy):
        merge_row(dy)

        @pl.when(y >= dy)
        def _():
            home_out[dy] = total_kv[dy].astype(BF16)
            home_copy(dy).start()

    send_home(2)
    settle(1)
    send_home(1)
    merge_row(0)
    finish(0)
    for dy in range(1, 3):

        @pl.when(y + dy < tall)
        def _():
            home_copy(dy).wait_recv()
            total_kv[0] = total_kv[0] + home_in[dy].astype(F32)

    gk[...] = total_kv[0, 0].astype(BF16)
    gv[...] = total_kv[0, 1].astype(BF16)

    finish(1)

    for one in low_copies + dlow_copies:
        one.wait_send()

    for dy in range(3):
        row_readers(dy, lambda copy: copy.wait_send())
    for dy in range(1, 3):

        @pl.when(y >= dy)
        def _():
            home_copy(dy).wait_send()

    @pl.when(y + 2 < tall)
    def _():
        column_copy(2).wait_send()

    for dy in range(1, 3):
        direct(dy, lambda copy: copy.wait_send())

    @pl.loop(0, earlier + 1)
    def _(e):
        forward(e).wait_send()

    for g in range(groups):
        sib_copy(g).wait_send()
    for e in range(units):
        if e % wide:
            to_x, copy = merge_copy(e)

            @pl.when(e <= earlier)
            def _():
                copy.wait_send()

    for kind in range(2):
        sent = got.at[kind, rest1]
        pltpu.make_async_copy(sent, sent, a1_send.at[kind]).wait()
        sent = red.at[kind, rest2]
        pltpu.make_async_copy(sent, sent, a2_send.at[kind]).wait()


def place_kernel(count, *refs):
    sems = refs[2 * count]
    copies = [
        pltpu.make_async_copy(refs[n], refs[count + n], sems.at[n]) for n in range(count)
    ]
    for one in copies:
        one.start()
    for one in copies:
        one.wait()


def on_device(
    hidden_rows, rotated_queries, rotated_keys, value_rows, adapter_down, adapter_up,
    output_gradient, document_blocks, document_adapter,
):
    seq = lax.axis_size("seq")
    mp = lax.axis_size("mp")
    rows, cols = hidden_rows.shape
    adapters = adapter_down.shape[0]
    units = seq // 4 + 1
    wide = seq // 8
    span = cols // 128
    groups = units // GROUP
    docs = document_blocks.shape[0]
    any_space = pl.BlockSpec(memory_space=pl.ANY)
    dma = pltpu.SemaphoreType.DMA
    vmem = pltpu.VMEM
    shapes = (
        jax.ShapeDtypeStruct((rows, cols), BF16),
        jax.ShapeDtypeStruct((rows, cols), BF16),
        jax.ShapeDtypeStruct((rows, HEAD), BF16),
        jax.ShapeDtypeStruct((rows, HEAD), BF16),
        jax.ShapeDtypeStruct((1, RANK, cols), F32),
        jax.ShapeDtypeStruct((1, RANK, cols), F32),
    )
    made = pl.pallas_call(
        functools.partial(kernel, seq, mp, docs),
        out_shape=[vmem(one.shape, one.dtype) for one in shapes],
        in_specs=[any_space] * 9,
        out_specs=[pl.BlockSpec(memory_space=pltpu.VMEM)] * 6,
        scratch_shapes=[
            pltpu.SMEM((docs,), jnp.int32),
            pltpu.SMEM((docs,), jnp.int32),
            vmem((rows, cols), BF16),
            vmem((rows, cols), BF16),
            vmem((adapters, RANK, cols), BF16),
            vmem((adapters, RANK, cols), BF16),
            vmem((rows, cols), BF16),
            vmem((units, 2, 2 * BLK, HEAD), BF16),
            vmem((cols, HEAD), BF16),
            vmem((HEAD, cols), BF16),
            vmem((cols, HEAD), BF16),
            vmem((HEAD, cols), BF16),
            vmem((units, 2 * BLK, cols), F32),
            vmem((units, 2 * BLK, cols), F32),
            vmem((units * 2 * BLK, cols), BF16),
            vmem((units * 2 * BLK, cols), BF16),
            vmem((mp, RANK, rows), F32),
            vmem((mp, RANK, rows), F32),
            vmem((24, cols), F32),
            vmem((16, cols), F32),
            vmem((units, HEAD, 2 * BLK), BF16),
            vmem((units, HEAD, 2 * BLK), BF16),
            vmem((2, GROUP * 2 * BLK, HEAD), F32),
            vmem((groups, GROUP, 2, BLK, HEAD), F32),
            vmem((groups, GROUP, 2, BLK, HEAD), BF16),
            vmem((groups, GROUP, 2, BLK, HEAD), BF16),
            vmem((units, 2, BLK, HEAD), BF16),
            vmem((3, wide, 2, BLK, HEAD), BF16),
            vmem((3, 2, BLK, HEAD), BF16),
            vmem((3, 2, BLK, HEAD), BF16),
            vmem((3, 2, BLK, HEAD), F32),
            vmem((adapters * RANK, span * RANK), BF16),
            vmem((2, span, RANK, 128), BF16),
            vmem((2, span * RANK, 128), BF16),
            vmem((2, seq * RANK, 128), BF16),
            vmem((2, seq * RANK, 128), BF16),
            dma((9,)),
            dma((mp,)), dma((mp,)), dma((mp,)), dma((mp,)),
            dma((3,)), dma((3, wide)), dma((3,)), dma((units,)), dma((units,)), dma((units,)),
            dma((groups,)), dma((groups,)), dma((units,)), dma((3, wide)),
            dma((3,)), dma((3,)),
            dma((2,)), dma((2,)), dma((2,)), dma((2,)),
        ],
        compiler_params=pltpu.CompilerParams(
            collective_id=0, has_side_effects=True, vmem_limit_bytes=48 * 1024 * 1024
        ),
    )(
        *(
            pltpu.with_memory_space_constraint(one, pltpu.HBM)
            for one in (
                document_blocks, document_adapter, hidden_rows, rotated_queries, rotated_keys,
                value_rows, adapter_down, adapter_up, output_gradient,
            )
        )
    )
    return pl.pallas_call(
        functools.partial(place_kernel, len(shapes)),
        out_shape=shapes,
        in_specs=[any_space] * len(shapes),
        out_specs=[any_space] * len(shapes),
        scratch_shapes=[dma((len(shapes),))],
    )(*(pltpu.with_memory_space_constraint(one, pltpu.VMEM) for one in made))


def solution(mesh):
    return jax.shard_map(
        on_device,
        mesh=mesh,
        in_specs=(
            P("seq", "mp"),
            P("seq", "mp"),
            P("seq", "mp"),
            P("seq", "mp"),
            P(None, None, "mp"),
            P(None, None, "mp"),
            P("seq", "mp"),
            P(),
            P(),
        ),
        out_specs=(
            P("seq", "mp"),
            P("seq", "mp"),
            P("seq", "mp"),
            P("seq", "mp"),
            P("seq", None, "mp"),
            P("seq", None, "mp"),
        ),
        check_vma=False,
    )
```

```python
import functools
import math

import jax
import jax.numpy as jnp
from jax import lax
from jax.experimental import pallas as pl
from jax.experimental.pallas import tpu as pltpu
from jax.sharding import PartitionSpec as P

HEAD = 128
BLK = 128
RANK = 16
NARROW = 256
GROUP = 3
NEG = -1e30
LOG2E = 1.4426950408889634
MESH = pl.DeviceIdType.MESH
F32 = jnp.float32
BF16 = jnp.bfloat16

NT = (((1,), (1,)), ((), ()))


def dot(a, b):
    return jnp.dot(a, b, preferred_element_type=F32)


def wrap(value, size):
    return jnp.where(value >= size, value - size, value)


def dot_nt(a, b):
    return lax.dot_general(a, b, NT, preferred_element_type=F32)


def kernel(
    seq, mp, docs,
    db_h, da_h, hid_h, rq_h, k_h, v_h, down_h, up_h, do_h,
    outv, gqv, gk, gv, ga, gb,
    db, da, hid, rq, down, up, do, kv, qs, qt, dos, dot_t, sbuf, dpbuf, pbuf, dsbuf,
    lowx, dlowx, stat, shifts, keys_t, vals_t, pair, own_st, sib_out, sib_in,
    dkv_out, dkv_in, home_out, home_in, total_kv, select, piece, got, red, fin,
    load_sem,
    low_send, low_recv, dlow_send, dlow_recv,
    col_send, row_send, direct_send, kv_recv, fwd_send, fwd_recv, sib_send, sib_recv, dkv_send, dkv_recv,
    home_send, home_recv,
    a1_send, a1_recv, a2_send, a2_recv,
):
    reach = seq // 4
    chips = seq // 2
    units = reach + 1
    wide = reach // 2
    tall = chips // wide
    cols = hid.shape[1]
    heads = cols // HEAD
    span = cols // 128
    groups = units // GROUP
    scale = 1.0 / math.sqrt(HEAD)
    fold = scale * LOG2E

    own = lax.axis_index("seq")
    m = lax.axis_index("mp")
    chip = own // 2
    core = own % 2
    sib = own + 1 - 2 * core
    mine = slice(0, BLK)
    other = slice(BLK, 2 * BLK)
    x = chip % wide
    y = chip // wide
    tier = span // 2
    place = (y % tier) * 2 + core
    level = y - y % tier

    def member(p):
        return ((level + p // 2) * wide + x) * 2 + p % 2
    earlier = jnp.minimum(reach, chip)

    def at_chip(to_x, to_y):
        return ((to_y * wide + to_x) * 2 + core, m)

    def load(src, dst, n):
        return pltpu.make_async_copy(src, dst, load_sem.at[n])

    loads = [
        load(k_h, kv.at[0, 0, mine], 0),
        load(v_h, kv.at[0, 1, mine], 1),
        load(hid_h, hid, 2),
        load(down_h, down, 3),
        load(up_h, up, 4),
        load(rq_h, rq, 5),
        load(do_h, do, 6),
        load(db_h, db, 7),
        load(da_h, da, 8),
    ]
    loads[0].start()
    loads[1].start()
    barrier = pltpu.get_barrier_semaphore()
    partners = [(own, wrap(m + step, mp)) for step in range(1, mp)]
    partners += [(sib, m)]
    partners += [at_chip(x, wrap(y + step, tall)) for step in range(1, tall)]
    partners += [(member(wrap(place + 2 * step + 1 - 2 * core, span)), m) for step in range(1, tier)]
    partners += [at_chip(wrap(x + step, wide), y) for step in range(1, wide)]
    for peer in partners:
        pl.semaphore_signal(barrier, inc=1, device_id=peer, device_id_type=MESH)
    skips = wide - 1
    greeted = len(partners)
    if skips:
        greeted += jnp.where(x == skips, jnp.minimum(2, tall - 1 - y), 0)
        for dy in range(1, 3):

            @pl.when(jnp.logical_and(x == 0, y >= dy))
            def _():
                pl.semaphore_signal(
                    barrier, inc=1, device_id=at_chip(skips, y - dy), device_id_type=MESH
                )

    for n in (7, 8, 2, 3, 6, 4, 5):
        loads[n].start()
    loads[0].wait()
    loads[1].wait()
    pl.semaphore_wait(barrier, greeted)

    def exchange(buf, send, recv):
        copies = []
        for step in sorted(range(1, mp), key=lambda step: abs(step - mp // 2)):
            peer = wrap(m + step, mp)
            copies.append(
                pltpu.make_async_remote_copy(
                    src_ref=buf.at[m], dst_ref=buf.at[m],
                    send_sem=send.at[step], recv_sem=recv.at[step],
                    device_id=(own, peer), device_id_type=MESH,
                )
            )
        return copies

    def column_copy(dy):
        return pltpu.make_async_remote_copy(
            src_ref=kv.at[0, :, mine], dst_ref=kv.at[dy * wide, :, mine],
            send_sem=col_send.at[dy], recv_sem=kv_recv.at[dy * wide],
            device_id=at_chip(x, y + dy), device_id_type=MESH,
        )

    def direct_copy(dy):
        e = dy * wide - skips
        return pltpu.make_async_remote_copy(
            src_ref=kv.at[0, :, mine], dst_ref=kv.at[e, :, mine],
            send_sem=direct_send.at[dy], recv_sem=kv_recv.at[e],
            device_id=at_chip(0, y + dy), device_id_type=MESH,
        )

    def direct(dy, act):
        if skips:

            @pl.when(jnp.logical_and(x == skips, y + dy < tall))
            def _():
                act(direct_copy(dy))

    def row_copy(dy, to_x):
        return pltpu.make_async_remote_copy(
            src_ref=kv.at[dy * wide, :, mine], dst_ref=kv.at[dy * wide + to_x - x, :, mine],
            send_sem=row_send.at[dy, to_x], recv_sem=kv_recv.at[dy * wide + to_x - x],
            device_id=at_chip(to_x, y), device_id_type=MESH,
        )

    def row_readers(dy, act):
        for to_x in range(wide):
            reads = (to_x > x, to_x != x, to_x < x)[dy]
            if dy and to_x == 0:
                reads = jnp.logical_and(reads, x != skips)

            @pl.when(jnp.logical_and(y >= dy, reads))
            def _():
                act(row_copy(dy, to_x))

    def kv_land(e):
        return pltpu.make_async_remote_copy(
            src_ref=kv.at[0, :, mine], dst_ref=kv.at[e, :, mine],
            send_sem=col_send.at[0], recv_sem=kv_recv.at[e],
            device_id=(sib, m), device_id_type=MESH,
        )

    def forward(e):
        return pltpu.make_async_remote_copy(
            src_ref=kv.at[e, :, mine], dst_ref=kv.at[e, :, other],
            send_sem=fwd_send.at[e], recv_sem=fwd_recv.at[e],
            device_id=(sib, m), device_id_type=MESH,
        )

    def forward_land(e):
        return pltpu.make_async_remote_copy(
            src_ref=kv.at[e, :, other], dst_ref=kv.at[e, :, other],
            send_sem=fwd_send.at[e], recv_sem=fwd_recv.at[e],
            device_id=(sib, m), device_id_type=MESH,
        )

    @pl.when(y + 1 < tall)
    def _():
        column_copy(1).start()

    forward(0).start()
    row_readers(0, lambda copy: copy.start())

    loads[7].wait()
    loads[8].wait()
    start = jnp.int32(0)
    first = jnp.int32(0)
    adapter = jnp.int32(0)
    bounds = []
    for d in range(docs):
        end = start + db[d]
        inside = jnp.logical_and(own >= start, own < end)
        first = jnp.where(inside, start, first)
        adapter = jnp.where(inside, da[d], adapter)
        bounds.append((start, end, da[d]))
        start = end

    loads[2].wait()
    loads[3].wait()
    lowx[m] = dot_nt(down[adapter], hid[...])
    low_copies = exchange(lowx, low_send, low_recv)
    for one in low_copies:
        one.start()

    @pl.when(y + 1 < tall)
    def _():
        column_copy(1).wait_send()

    @pl.when(y + 2 < tall)
    def _():
        column_copy(2).start()

    for dy in range(1, 3):
        direct(dy, lambda copy: copy.start())
    loads[6].wait()
    for h in range(heads):
        here = slice(h * BLK, (h + 1) * BLK)
        part = do[:, h * HEAD : (h + 1) * HEAD]
        dos[here, :] = part
        dot_t[:, here] = part.T

    size = select.shape
    row = lax.broadcasted_iota(jnp.int32, size, 0)
    col = lax.broadcasted_iota(jnp.int32, size, 1)
    same = (row % RANK) == (col % RANK)
    row_a = row // RANK
    col_s = member(col // RANK)
    hit = jnp.zeros(size, F32)
    for begin, end, name in bounds:
        inside = jnp.logical_and(col_s >= begin, col_s < end)
        inside = jnp.logical_and(inside, row_a == name)
        hit = jnp.where(jnp.logical_and(inside, same), 1.0, hit)
    select[...] = hit.astype(BF16)

    @pl.loop(earlier + 1, units)
    def _(e):
        kv[e] = jnp.zeros(kv.shape[1:], BF16)

    for dy in range(1, 3):

        @pl.when(y >= dy)
        def _():
            kv_land(dy * wide).wait_recv()
            forward(dy * wide).start()

        row_readers(dy, lambda copy: copy.start())

    @pl.loop(1, x + 1)
    def _(e):
        kv_land(e).wait_recv()
        forward(e).start()

    loads[4].wait()
    loads[5].wait()
    up_rows = up[adapter]
    for one in low_copies:
        one.wait_recv()
    low_sum = lowx[0]
    for step in range(1, mp):
        low_sum = low_sum + lowx[step]
    low_t = low_sum.astype(BF16)
    low = low_sum.T.astype(BF16)
    for h in range(heads):
        part = slice(h * HEAD, (h + 1) * HEAD)
        here = slice(h * BLK, (h + 1) * BLK)
        q = (rq[:, part].astype(F32) + dot(low, up_rows[:, part])).astype(BF16)
        qs[here, :] = q
        qt[:, here] = q.T

    below = lax.broadcasted_iota(jnp.int32, (BLK, cols), 0) <= (
        lax.broadcasted_iota(jnp.int32, (BLK, cols), 1) % BLK
    )
    turn_of = {}

    def score(turn, halves):
        keys = jnp.concatenate([kv[e, 0, h * BLK : (h + 1) * BLK] for e, h in halves], axis=0)
        values = jnp.concatenate([kv[e, 1, h * BLK : (h + 1) * BLK] for e, h in halves], axis=0)
        s_all = dot(keys, qt[...])
        dp_all = dot(values, dot_t[...])
        keys_all = keys.T
        values_all = values.T
        parts = []
        top = None if turn == 0 else stat[0:1, :]
        for n, (e, h) in enumerate(halves):
            turn_of[e, h] = turn
            here = slice(n * BLK, (n + 1) * BLK)
            half = slice(h * BLK, (h + 1) * BLK)
            keys_t[e, :, half] = keys_all[:, here]
            vals_t[e, :, half] = values_all[:, here]
            block = 2 * (chip - e) + (core if h == 0 else 1 - core)
            seen = jnp.logical_and(block >= first, block <= own)
            s = s_all[here]
            if e == 0 and h == 0:
                s = jnp.where(below, s, NEG)
            off = jnp.where(seen, 0.0, -NEG)
            high = jnp.max(s, axis=0, keepdims=True) - off
            top = high if top is None else jnp.maximum(top, high)
            parts.append((e, half, s, dp_all[here], off))
        shift = top * fold
        total = delta = None
        if turn:
            shrink = jnp.exp2(stat[0:1, :] * fold - shift)
            total = shrink * stat[8:9, :]
            delta = shrink * stat[16:17, :]
        for e, half, s, dp, off in parts:
            p = jnp.exp2(s * fold - (shift + off))
            sbuf[e, half, :] = p
            dpbuf[e, half, :] = dp
            row_sum = jnp.sum(p, axis=0, keepdims=True)
            row_delta = jnp.sum(p * dp, axis=0, keepdims=True)
            total = row_sum if total is None else total + row_sum
            delta = row_delta if delta is None else delta + row_delta
        stat[0:1, :] = top
        stat[8:9, :] = total
        stat[16:17, :] = delta
        shifts[turn : turn + 1, :] = shift

    forward_land(0).wait_recv()
    for dy in range(1, 3):

        @pl.when(y >= dy)
        def _():
            forward_land(dy * wide).wait_recv()

    score(0, [(dy * wide, h) for dy in range(3) for h in range(2)])
    turns = 1
    for dy in range(2):
        near = [dy * wide + step for step in range(1, wide)]
        for e in near:

            @pl.when(jnp.logical_and(e > x, e <= earlier))
            def _():
                kv_land(e).wait_recv()
                forward(e).start()

        if near:
            score(turns, [(e, 0) for e in near])
        for e in near:

            @pl.when(e <= earlier)
            def _():
                forward_land(e).wait_recv()

        if near:
            score(turns + 1, [(e, 1) for e in near])
        turns += 2

    total = stat[8:9, :]
    shifts[8:16, :] = jnp.exp2(
        shifts[0:8, :] - (stat[0:1, :] * fold + jnp.log(total) * LOG2E)
    )
    stat[16:17, :] = stat[16:17, :] / total
    for e in range(units):
        for h in range(2):
            half = slice(h * BLK, (h + 1) * BLK)
            here = slice((2 * e + h) * BLK, (2 * e + h + 1) * BLK)
            factor = 8 + turn_of[e, h]
            for at in range(0, cols, NARROW):
                part = slice(at, at + NARROW)
                p = sbuf[e, half, part] * shifts[factor : factor + 1, part]
                ds = p * (dpbuf[e, half, part] - stat[16:17, part])
                dsbuf[here, part] = ds.astype(BF16)

    def all_units(turned):
        return jnp.concatenate([turned[e] for e in range(units)], axis=1)

    dq_t = dot(all_units(keys_t), dsbuf[...]) * scale
    for h in range(heads):
        part = slice(h * HEAD, (h + 1) * HEAD)
        gqv[:, part] = dq_t[:, h * BLK : (h + 1) * BLK].T.astype(BF16)
    dlowx[m] = dot_nt(up_rows, gqv[...])
    dlow_copies = exchange(dlowx, dlow_send, dlow_recv)
    for one in dlow_copies:
        one.start()

    own16 = pl.ds(pl.multiple_of(own * RANK, RANK), RANK)
    place16 = pl.ds(pl.multiple_of(place * RANK, RANK), RANK)
    rest1 = pl.ds(0, (span - 1) * RANK)
    rest2 = pl.ds(0, (seq - 1) * RANK)

    def spread(kind, product):
        for t in range(span):
            piece[kind, t] = product[:, t * 128 : (t + 1) * 128].astype(BF16)

        for step in sorted(range(1, span), key=lambda step: abs(step - span // 2)):
            peer = wrap(place + step, span)
            pltpu.make_async_remote_copy(
                src_ref=piece.at[kind, peer], dst_ref=got.at[kind, place16],
                send_sem=a1_send.at[kind], recv_sem=a1_recv.at[kind],
                device_id=(member(peer), m), device_id_type=MESH,
            ).start()

    def settle(kind):
        land = got.at[kind, rest1]
        pltpu.make_async_copy(land, land, a1_recv.at[kind]).wait()
        got[kind, place16, :] = piece[kind, place]
        red[kind] = dot(select[...], got[kind]).astype(BF16)

        for step in sorted(range(1, seq), key=lambda step: abs(step - seq // 2 - wide // 2)):
            peer = own + step
            peer = jnp.where(peer >= seq, peer - seq, peer)
            pltpu.make_async_remote_copy(
                src_ref=red.at[kind, pl.ds(pl.multiple_of(peer * RANK, RANK), RANK)],
                dst_ref=fin.at[kind, own16],
                send_sem=a2_send.at[kind], recv_sem=a2_recv.at[kind],
                device_id=(peer, m), device_id_type=MESH,
            ).start()

    def finish(kind):
        land = fin.at[kind, rest2]
        pltpu.make_async_copy(land, land, a2_recv.at[kind]).wait()
        fin[kind, own16, :] = red[kind, own16, :]
        for t in range(span):
            whole = jnp.zeros((RANK, 128), F32)
            for line in range(seq // span):
                line_y = line // wide * tier + t // 2
                at = ((line_y * wide + line % wide) * 2 + t % 2) * RANK
                whole = whole + fin[kind, at : at + RANK, :].astype(F32)
            (gb, ga)[kind][0, :, t * 128 : (t + 1) * 128] = whole

    def sib_copy(g):
        return pltpu.make_async_remote_copy(
            src_ref=sib_out.at[g], dst_ref=sib_in.at[g],
            send_sem=sib_send.at[g], recv_sem=sib_recv.at[g],
            device_id=(sib, m), device_id_type=MESH,
        )

    def merge_copy(e):
        owner = chip - e
        to_x = owner % wide
        dy = y - owner // wide
        return to_x, pltpu.make_async_remote_copy(
            src_ref=dkv_out.at[e], dst_ref=dkv_in.at[dy, x],
            send_sem=dkv_send.at[e], recv_sem=dkv_recv.at[dy, x],
            device_id=at_chip(to_x, y), device_id_type=MESH,
        )

    def merge_land(dy, from_x):
        return pltpu.make_async_remote_copy(
            src_ref=dkv_out.at[0], dst_ref=dkv_in.at[dy, from_x],
            send_sem=dkv_send.at[0], recv_sem=dkv_recv.at[dy, from_x],
            device_id=(sib, m), device_id_type=MESH,
        )

    def home_copy(dy):
        return pltpu.make_async_remote_copy(
            src_ref=home_out.at[dy], dst_ref=home_in.at[dy],
            send_sem=home_send.at[dy], recv_sem=home_recv.at[dy],
            device_id=at_chip(x, y - dy), device_id_type=MESH,
        )

    def merge_row(dy):
        for from_x in range(wide):
            writes = (from_x > x, from_x != x, from_x < x)[dy]

            @pl.when(jnp.logical_and(y >= dy, writes))
            def _():
                merge_land(dy, from_x).wait_recv()
                total_kv[dy] = total_kv[dy] + dkv_in[dy, from_x].astype(F32)

    def fix(g):
        for e in range(g * GROUP, (g + 1) * GROUP):
            for h in range(2):
                half = slice(h * BLK, (h + 1) * BLK)
                here = slice((2 * e + h) * BLK, (2 * e + h + 1) * BLK)
                factor = 8 + turn_of[e, h]
                for at in range(0, cols, NARROW):
                    part = slice(at, at + NARROW)
                    p = sbuf[e, half, part] * shifts[factor : factor + 1, part]
                    pbuf[here, part] = p.astype(BF16)

    def weigh(g):
        fix(g)
        here = slice(g * GROUP * 2 * BLK, (g + 1) * GROUP * 2 * BLK)
        pair[0] = dot(dsbuf[here, :], qs[...]) * scale
        pair[1] = dot(pbuf[here, :], dos[...])
        for k in range(GROUP):
            for kind in range(2):
                at = 2 * k * BLK
                own_st[g, k, kind] = pair[kind, at : at + BLK, :]
                sib_out[g, k, kind] = pair[kind, at + BLK : at + 2 * BLK, :].astype(BF16)
        sib_copy(g).start()

    def pass_on(g):
        sib_copy(g).wait_recv()
        for k in range(GROUP - 1, -1, -1):
            e = g * GROUP + k
            merged = own_st[g, k] + sib_in[g, k].astype(F32)
            if e % wide == 0:
                total_kv[e // wide] = merged
            else:
                dkv_out[e] = merged.astype(BF16)
                to_x, copy = merge_copy(e)

                @pl.when(e <= earlier)
                def _():
                    copy.start()

    for g in range(groups - 1, -1, -1):
        weigh(g)
        if g == groups - 2 or groups == 1:
            spread(0, dot(low_t, gqv[...]))
        if g < groups - 1:
            pass_on(g + 1)
    pass_on(0)

    for one in dlow_copies:
        one.wait_recv()
    dlow_sum = dlowx[0]
    for step in range(1, mp):
        dlow_sum = dlow_sum + dlowx[step]
    spread(1, dot(dlow_sum.astype(BF16), hid[...]))
    settle(0)

    out_t = dot(all_units(vals_t), pbuf[...])
    for h in range(heads):
        part = slice(h * HEAD, (h + 1) * HEAD)
        outv[:, part] = out_t[:, part].T.astype(BF16)

    def send_home(dy):
        merge_row(dy)

        @pl.when(y >= dy)
        def _():
            home_out[dy] = total_kv[dy].astype(BF16)
            home_copy(dy).start()

    send_home(2)
    settle(1)
    send_home(1)
    merge_row(0)
    finish(0)
    for dy in range(1, 3):

        @pl.when(y + dy < tall)
        def _():
            home_copy(dy).wait_recv()
            total_kv[0] = total_kv[0] + home_in[dy].astype(F32)

    gk[...] = total_kv[0, 0].astype(BF16)
    gv[...] = total_kv[0, 1].astype(BF16)

    finish(1)

    for one in low_copies + dlow_copies:
        one.wait_send()

    for dy in range(3):
        row_readers(dy, lambda copy: copy.wait_send())
    for dy in range(1, 3):

        @pl.when(y >= dy)
        def _():
            home_copy(dy).wait_send()

    @pl.when(y + 2 < tall)
    def _():
        column_copy(2).wait_send()

    for dy in range(1, 3):
        direct(dy, lambda copy: copy.wait_send())

    @pl.loop(0, earlier + 1)
    def _(e):
        forward(e).wait_send()

    for g in range(groups):
        sib_copy(g).wait_send()
    for e in range(units):
        if e % wide:
            to_x, copy = merge_copy(e)

            @pl.when(e <= earlier)
            def _():
                copy.wait_send()

    for kind in range(2):
        sent = got.at[kind, rest1]
        pltpu.make_async_copy(sent, sent, a1_send.at[kind]).wait()
        sent = red.at[kind, rest2]
        pltpu.make_async_copy(sent, sent, a2_send.at[kind]).wait()


def place_kernel(count, *refs):
    sems = refs[2 * count]
    copies = [
        pltpu.make_async_copy(refs[n], refs[count + n], sems.at[n]) for n in range(count)
    ]
    for one in copies:
        one.start()
    for one in copies:
        one.wait()


def on_device(
    hidden_rows, rotated_queries, rotated_keys, value_rows, adapter_down, adapter_up,
    output_gradient, document_blocks, document_adapter,
):
    seq = lax.axis_size("seq")
    mp = lax.axis_size("mp")
    rows, cols = hidden_rows.shape
    adapters = adapter_down.shape[0]
    units = seq // 4 + 1
    wide = seq // 8
    span = cols // 128
    groups = units // GROUP
    docs = document_blocks.shape[0]
    any_space = pl.BlockSpec(memory_space=pl.ANY)
    dma = pltpu.SemaphoreType.DMA
    vmem = pltpu.VMEM
    shapes = (
        jax.ShapeDtypeStruct((rows, cols), BF16),
        jax.ShapeDtypeStruct((rows, cols), BF16),
        jax.ShapeDtypeStruct((rows, HEAD), BF16),
        jax.ShapeDtypeStruct((rows, HEAD), BF16),
        jax.ShapeDtypeStruct((1, RANK, cols), F32),
        jax.ShapeDtypeStruct((1, RANK, cols), F32),
    )
    made = pl.pallas_call(
        functools.partial(kernel, seq, mp, docs),
        out_shape=[vmem(one.shape, one.dtype) for one in shapes],
        in_specs=[any_space] * 9,
        out_specs=[pl.BlockSpec(memory_space=pltpu.VMEM)] * 6,
        scratch_shapes=[
            pltpu.SMEM((docs,), jnp.int32),
            pltpu.SMEM((docs,), jnp.int32),
            vmem((rows, cols), BF16),
            vmem((rows, cols), BF16),
            vmem((adapters, RANK, cols), BF16),
            vmem((adapters, RANK, cols), BF16),
            vmem((rows, cols), BF16),
            vmem((units, 2, 2 * BLK, HEAD), BF16),
            vmem((cols, HEAD), BF16),
            vmem((HEAD, cols), BF16),
            vmem((cols, HEAD), BF16),
            vmem((HEAD, cols), BF16),
            vmem((units, 2 * BLK, cols), F32),
            vmem((units, 2 * BLK, cols), F32),
            vmem((units * 2 * BLK, cols), BF16),
            vmem((units * 2 * BLK, cols), BF16),
            vmem((mp, RANK, rows), F32),
            vmem((mp, RANK, rows), F32),
            vmem((24, cols), F32),
            vmem((16, cols), F32),
            vmem((units, HEAD, 2 * BLK), BF16),
            vmem((units, HEAD, 2 * BLK), BF16),
            vmem((2, GROUP * 2 * BLK, HEAD), F32),
            vmem((groups, GROUP, 2, BLK, HEAD), F32),
            vmem((groups, GROUP, 2, BLK, HEAD), BF16),
            vmem((groups, GROUP, 2, BLK, HEAD), BF16),
            vmem((units, 2, BLK, HEAD), BF16),
            vmem((3, wide, 2, BLK, HEAD), BF16),
            vmem((3, 2, BLK, HEAD), BF16),
            vmem((3, 2, BLK, HEAD), BF16),
            vmem((3, 2, BLK, HEAD), F32),
            vmem((adapters * RANK, span * RANK), BF16),
            vmem((2, span, RANK, 128), BF16),
            vmem((2, span * RANK, 128), BF16),
            vmem((2, seq * RANK, 128), BF16),
            vmem((2, seq * RANK, 128), BF16),
            dma((9,)),
            dma((mp,)), dma((mp,)), dma((mp,)), dma((mp,)),
            dma((3,)), dma((3, wide)), dma((3,)), dma((units,)), dma((units,)), dma((units,)),
            dma((groups,)), dma((groups,)), dma((units,)), dma((3, wide)),
            dma((3,)), dma((3,)),
            dma((2,)), dma((2,)), dma((2,)), dma((2,)),
        ],
        compiler_params=pltpu.CompilerParams(
            collective_id=0, has_side_effects=True, vmem_limit_bytes=48 * 1024 * 1024
        ),
    )(
        *(
            pltpu.with_memory_space_constraint(one, pltpu.HBM)
            for one in (
                document_blocks, document_adapter, hidden_rows, rotated_queries, rotated_keys,
                value_rows, adapter_down, adapter_up, output_gradient,
            )
        )
    )
    return pl.pallas_call(
        functools.partial(place_kernel, len(shapes)),
        out_shape=shapes,
        in_specs=[any_space] * len(shapes),
        out_specs=[any_space] * len(shapes),
        scratch_shapes=[dma((len(shapes),))],
    )(*(pltpu.with_memory_space_constraint(one, pltpu.VMEM) for one in made))


def solution(mesh):
    return jax.shard_map(
        on_device,
        mesh=mesh,
        in_specs=(
            P("seq", "mp"),
            P("seq", "mp"),
            P("seq", "mp"),
            P("seq", "mp"),
            P(None, None, "mp"),
            P(None, None, "mp"),
            P("seq", "mp"),
            P(),
            P(),
        ),
        out_specs=(
            P("seq", "mp"),
            P("seq", "mp"),
            P("seq", "mp"),
            P("seq", "mp"),
            P("seq", None, "mp"),
            P("seq", None, "mp"),
        ),
        check_vma=False,
    )
```
